256 devices in a mesh: row: 16 (over z_lo, y, core), col: 16 (over z_hi, x).
Axes of the slice: x: 4, y: 4, z: 8 (z_hi: 4, z_lo: 2; z = z_hi * 2 + z_lo), core: 2. Of those that a mesh axis runs over, the one named last changes fastest.
Arguments:
- states_now: float32 [40, 32768], P(None, ('col', 'row')), may hold values from -60 to 60
- states_next: float32 [40, 32768], P(None, ('row', 'col')), may hold values from -60 to 60
- states_last: float32 [40, 32768], P(None, ('col', 'row')), may hold values from -60 to 60
- payoff_now: bfloat16 [64, 32768], P(None, ('col', 'row')), may hold values from 0 to 2
- payoff_next: bfloat16 [64, 32768], P(None, ('row', 'col')), may hold values from 0 to 2
- payoff_last: bfloat16 [64, 32768], P(None, ('col', 'row')), may hold values from 0 to 2
Outputs:
- value_next: float32 [64, 32768], P(None, ('row', 'col'))
- value_now: float32 [64, 32768], P(None, ('col', 'row'))
The draws below stay inside these ranges and needn't reach their ends.
All inputs are finite; a program needn't handle non-finite values.
Results may differ from the reference program's by a relative error of at most 0.0003.
Values sent between devices are 32-bit elements; how exact they have to be, the bound alone decides.
A program may use at most 128 MiB of HBM per device.

```python
import math
import jax
import jax.numpy as jnp
from jax import lax

F = 40
SWAPS = 64
MESH_PTS = 32768


def draw_mesh(key):
    grid_shape = (3, F, MESH_PTS)
    points = 0.55 * jax.random.truncated_normal(jax.random.fold_in(key, 7), -6.0, 6.0, grid_shape, jnp.float32)
    return points


def draw_states_now(key, part):
    return draw_mesh(key)[0]


def draw_states_next(key, part):
    return draw_mesh(key)[1]


def draw_states_last(key, part):
    return draw_mesh(key)[2]


def levels(rng, dims, cuts, smallest, largest):
    factor_of, own = 1.0, jax.random.fold_in(rng, 6)
    for axis_at, shards_of in cuts:
        draws = jnp.exp(jax.random.uniform(jax.random.fold_in(own, axis_at), (shards_of,), jnp.float32, smallest / len(cuts), largest / len(cuts)))
        factor_of = factor_of * jnp.repeat(draws, dims[axis_at] // shards_of).reshape([-1 if axis == axis_at else 1 for axis in range(len(dims))])
    return factor_of


def setup_inputs(seed: int = 0) -> dict:
    seeds = jax.random.split(jax.random.key(seed), 7)
    return {
        "states_now": draw_states_now(jax.random.fold_in(seeds[6], 71), 0),
        "states_next": draw_states_next(jax.random.fold_in(seeds[6], 71), 0),
        "states_last": draw_states_last(jax.random.fold_in(seeds[6], 71), 0),
        "payoff_now": jnp.clip(2.0 * jax.random.uniform(seeds[3], (SWAPS, MESH_PTS), jnp.float32) ** levels(seeds[3], (SWAPS, MESH_PTS), ((1, 256),), -0.2, 0.2), 0.0, 2.0).astype(jnp.bfloat16),
        "payoff_next": jnp.clip(2.0 * jax.random.uniform(seeds[4], (SWAPS, MESH_PTS), jnp.float32) ** levels(seeds[4], (SWAPS, MESH_PTS), ((1, 256),), -0.2, 0.2), 0.0, 2.0).astype(jnp.bfloat16),
        "payoff_last": jnp.clip(2.0 * jax.random.uniform(seeds[5], (SWAPS, MESH_PTS), jnp.float32) ** levels(seeds[5], (SWAPS, MESH_PTS), ((1, 256),), -0.2, 0.2), 0.0, 2.0).astype(jnp.bfloat16),
    }


def backward(earlier, later, later_value, payoff):
    factors, points = earlier.shape
    swaps = later_value.shape[0]
    block_cols = math.gcd(points, 1024)
    block_count = points // block_cols
    row_norms = jnp.sum(earlier * earlier, axis=0)
    col_blocks = later.reshape(factors, block_count, block_cols).transpose(1, 0, 2)
    value_blocks = later_value.reshape(swaps, block_count, block_cols).transpose(1, 0, 2)

    def update(running, block_item):
        col_states, col_values = block_item
        col_norms = jnp.sum(col_states * col_states, axis=0)
        cross_term = jnp.dot(earlier.T, col_states, precision=lax.Precision.HIGHEST, preferred_element_type=jnp.float32)
        log_weight = cross_term - 0.5 * row_norms[:, None] - 0.5 * col_norms[None, :]
        col_peak = jnp.max(log_weight, axis=0)
        shifted = jnp.exp(log_weight - col_peak[None, :])
        density = jnp.sum(shifted, axis=0)
        kernel = shifted.astype(jnp.bfloat16)
        scaled = (col_values / density[None, :]).astype(jnp.bfloat16)
        return running + jnp.dot(scaled, kernel.T, preferred_element_type=jnp.float32), None

    initial = jnp.zeros((swaps, points), jnp.float32)
    continuation, ignored = lax.scan(update, initial, (col_blocks, value_blocks))
    return jnp.maximum(payoff.astype(jnp.float32), continuation)


def reference(states_now, states_next, states_last, payoff_now, payoff_next, payoff_last):
    value_next = backward(states_next, states_last, payoff_last.astype(jnp.float32), payoff_next)
    value_now = backward(states_now, states_next, value_next, payoff_now)
    return value_next, value_now
```

```python
import jax
import jax.numpy as jnp
from jax import lax
from jax.experimental import pallas as pl
from jax.experimental.pallas import tpu as pltpu
from jax.sharding import PartitionSpec as P

F32, BF16 = jnp.float32, jnp.bfloat16
W = 128
SIDE = 16
QUAD = 4
HALF = 8
MESH = pl.DeviceIdType.MESH


def span(block, width):
    return pl.ds(pl.multiple_of(block * width, width), width)


def loop(count, body):
    def step(k, carry):
        body(k)
        return carry

    lax.fori_loop(0, count, step, 0)


def split3(v):
    high = v.astype(BF16).astype(F32)
    rest = v - high
    mid = rest.astype(BF16).astype(F32)
    return high, mid, rest - mid


def operand(block, earlier):
    high, mid, low = split3(block)
    norm = split3(-0.5 * jnp.sum(block * block, axis=0, keepdims=True))
    row = lax.broadcasted_iota(jnp.int32, (8, block.shape[1]), 0)
    extra = jnp.where(row < 6, 1.0, 0.0)
    for k in range(3):
        extra = jnp.where(row == (k if earlier else k + 3), norm[k], extra)
    pieces = (high, high, mid, mid, high, low) if earlier else (high, mid, high, mid, low, high)
    return jnp.concatenate(pieces + (extra, jnp.zeros_like(extra)), axis=0)


def build_later(states, later):
    def one(k):
        later[:, span(k, W)] = operand(states[k], False).astype(BF16)

    loop(SIDE, one)


def build_earlier(states, earlier):
    def one(k):
        earlier[span(k, W), :] = operand(states[k], True).T.astype(BF16)

    loop(SIDE, one)


def log_pass(earlier, later, log_kernel, peak):
    rows, cols = 256, 256

    def col(jc):
        js = span(jc, cols)

        def row(ic, top):
            i = span(ic, rows)
            tile = jnp.dot(earlier[i, :], later[:, js], preferred_element_type=F32)
            log_kernel[i, js] = tile
            return jnp.maximum(top, jnp.max(tile.reshape(rows // 8, 8, cols), axis=0))

        count = log_kernel.shape[0] // rows
        top = lax.fori_loop(0, count, row, jnp.full((8, cols), -jnp.inf, F32), unroll=True)
        peak[:, js] = jnp.max(top, axis=0, keepdims=True)

    loop(log_kernel.shape[1] // cols, col)


def exp_pass(log_kernel, kernel, peak, density):
    rows, cols = 64, 256

    def col(jc):
        js = span(jc, cols)
        top = jnp.broadcast_to(peak[:, js], (8, cols))

        def row(ic, total):
            i = span(ic, rows)
            tile = jnp.exp(log_kernel[i, js].reshape(rows // 8, 8, cols) - top[None])
            kernel[i, js] = tile.reshape(rows, cols).astype(BF16)
            return total + jnp.sum(tile, axis=0)

        count = log_kernel.shape[0] // rows
        total = lax.fori_loop(0, count, row, jnp.zeros((8, cols), F32), unroll=4)
        density[:, js] = jnp.sum(total, axis=0, keepdims=True)

    loop(log_kernel.shape[1] // cols, col)


def remote(src, dst, send, recv, row, col):
    return pltpu.make_async_remote_copy(
        src_ref=src, dst_ref=dst, send_sem=send, recv_sem=recv, device_id=(row, col), device_id_type=MESH
    )


def wait_for(ref, sem):
    pltpu.make_async_copy(ref, ref, sem).wait()


class Place:
    def __init__(self):
        self.row, self.col = lax.axis_index("row"), lax.axis_index("col")
        self.chip, self.core = self.row // 2, self.row % 2
        self.z, self.x = self.col // QUAD, self.col % QUAD
        self.twin = self.chip * 2 + 1 - self.core

    def on_core(self, k):
        return ((self.chip + k) % HALF) * 2 + self.core

    def along_z(self, k):
        return ((self.z + k) % QUAD) * QUAD + self.x

    def along_x(self, k):
        return self.z * QUAD + (self.x + k) % QUAD


def row_send(me, own, buf, send, recv):
    def one(k):
        remote(own, buf.at[me.row], send, recv.at[me.row], me.on_core(k + 1), me.col).start()

    loop(HALF - 1, one)
    remote(own, buf.at[me.row], send, recv.at[me.row], me.twin, me.col).start()


def row_relay(me, buf, send, recv):
    def one(k):
        slot = me.on_core(HALF - 1 - k)
        wait_for(buf.at[slot], recv.at[slot])
        remote(buf.at[slot], buf.at[slot], send, recv.at[slot], me.twin, me.col).start()

    loop(HALF - 1, one)


def row_finish(me, buf, recv):
    def one(k):
        slot = k * 2 + 1 - me.core
        wait_for(buf.at[slot], recv.at[slot])

    loop(HALF, one)


def col_send(me, own, buf, send, recv):
    def one(k):
        remote(own, buf.at[me.col], send, recv.at[me.col], me.row, me.along_z(k + 1)).start()

    loop(QUAD - 1, one)

    def two(k):
        remote(own, buf.at[me.col], send, recv.at[me.col], me.row, me.along_x(k + 1)).start()

    loop(QUAD - 1, two)


def col_relay(me, buf, send, recv):
    def one(k):
        slot = me.along_z(QUAD - 1 - k)
        wait_for(buf.at[slot], recv.at[slot])

        def two(q):
            remote(buf.at[slot], buf.at[slot], send, recv.at[slot], me.row, me.along_x(q + 1)).start()

        loop(QUAD - 1, two)

    loop(QUAD - 1, one)


def col_finish(me, buf, recv):
    def one(k):
        def two(q):
            slot = k * QUAD + (me.x + q + 1) % QUAD
            wait_for(buf.at[slot], recv.at[slot])

        loop(QUAD - 1, two)

    loop(QUAD, one)


def stat_send(me, buf, send, recv):
    own = buf.at[me.row]

    def one(k):
        remote(own, own, send, recv, (me.row + k + 1) % SIDE, me.col).start()

    loop(SIDE - 1, one)


def stat_finish(buf, recv, out, combine):
    wait_for(buf.at[pl.ds(0, SIDE - 1)], recv)
    total = buf[0]
    for k in range(1, SIDE):
        total = combine(total, buf[k])
    out[...] = total


def product_send(me, scaled, kernel, part, arrived, send, recv):
    def zs(k):
        z = (me.z + k + 1) % QUAD

        def xs(q):
            x = (me.x + q + 1) % QUAD
            slot = z * QUAD + x
            rows = kernel[span(slot, W), :]
            part[slot] = lax.dot_general(
                scaled[...], rows, (((1,), (1,)), ((), ())), preferred_element_type=F32
            )
            return x, slot

        def away(q):
            x, slot = xs(q)
            remote(part.at[slot], arrived.at[z, me.x], send, recv.at[z], me.row, me.z * QUAD + x).start()

        loop(QUAD - 1, away)
        x, slot = xs(QUAD - 1)
        arrived[z, me.x] = part[slot]

    loop(QUAD, zs)


def sum_send(me, arrived, sums, final, send, recv_x, recv_z):
    def one(k):
        z = (me.z + k + 1) % QUAD
        wait_for(arrived.at[z, pl.ds(0, QUAD - 1)], recv_x.at[z])
        sums[z] = arrived[z, 0] + arrived[z, 1] + arrived[z, 2] + arrived[z, 3]
        remote(sums.at[z], final.at[me.z], send, recv_z, me.row, z * QUAD + me.x).start()

    loop(QUAD - 1, one)
    wait_for(arrived.at[me.z, pl.ds(0, QUAD - 1)], recv_x.at[me.z])
    final[me.z] = arrived[me.z, 0] + arrived[me.z, 1] + arrived[me.z, 2] + arrived[me.z, 3]


def sum_finish(final, recv_z):
    wait_for(final.at[pl.ds(0, QUAD - 1)], recv_z)
    return final[0] + final[1] + final[2] + final[3]


def kernel_body(
    now_ref, next_ref, last_ref, pay_now, pay_next, pay_last, out_next, out_now,
    x1, y1, x2, y2, v1, v2, own_v,
    earlier1, later1, earlier2, later2, log1, log2, kern, scaled,
    peaks1, dens1, peaks2, dens2, peak, density1, density2, stat_row,
    part1, arrived1, sums1, final1, part2, arrived2, sums2, final2,
    own_sem, gather_send, stat_send_sem, sum_send_x, sum_send_z,
    recv_gather, recv_stat, recv_x, recv_z,
):
    me = Place()

    barrier = pltpu.get_barrier_semaphore()

    def greet_row(k):
        pl.semaphore_signal(barrier, inc=1, device_id=((me.row + k + 1) % SIDE, me.col), device_id_type=MESH)

    loop(SIDE - 1, greet_row)

    def greet_col(k):
        pl.semaphore_signal(barrier, inc=1, device_id=(me.row, me.along_z(k + 1)), device_id_type=MESH)
        pl.semaphore_signal(barrier, inc=1, device_id=(me.row, me.along_x(k + 1)), device_id_type=MESH)

    loop(QUAD - 1, greet_col)

    own = [
        pltpu.make_async_copy(next_ref, x1.at[me.col], own_sem.at[0]),
        pltpu.make_async_copy(last_ref, y1.at[me.row], own_sem.at[1]),
        pltpu.make_async_copy(now_ref, x2.at[me.col], own_sem.at[2]),
        pltpu.make_async_copy(next_ref, y2.at[me.row], own_sem.at[3]),
    ]
    for copy in own:
        copy.start()
    own_v[0] = pay_last[...].astype(F32)
    v1[me.row] = own_v[0]
    for copy in own:
        copy.wait()
    pl.semaphore_wait(barrier, SIDE - 1 + 2 * (QUAD - 1))

    g = lambda k: (gather_send.at[k], recv_gather.at[k])
    col_send(me, next_ref, x1, *g(0))
    row_send(me, last_ref, y1, *g(1))
    col_relay(me, x1, *g(0))
    row_relay(me, y1, *g(1))
    col_send(me, now_ref, x2, *g(2))
    row_send(me, next_ref, y2, *g(3))
    row_send(me, own_v.at[0], v1, *g(4))
    row_finish(me, y1, recv_gather.at[1])
    build_later(y1, later1)
    col_finish(me, x1, recv_gather.at[0])
    build_earlier(x1, earlier1)

    log_pass(earlier1, later1, log1, stat_row)
    peaks1[me.row] = stat_row[...]
    stat_send(me, peaks1, stat_send_sem.at[0], recv_stat.at[0])

    col_relay(me, x2, *g(2))
    row_relay(me, y2, *g(3))
    row_relay(me, v1, *g(4))

    stat_finish(peaks1, recv_stat.at[0], peak, jnp.maximum)
    exp_pass(log1, kern, peak, stat_row)
    dens1[me.row] = stat_row[...]
    stat_send(me, dens1, stat_send_sem.at[1], recv_stat.at[1])

    row_finish(me, y2, recv_gather.at[3])
    build_later(y2, later2)
    col_finish(me, x2, recv_gather.at[2])
    build_earlier(x2, earlier2)
    row_finish(me, v1, recv_gather.at[4])

    stat_finish(dens1, recv_stat.at[1], density1, jnp.add)

    def scale(values, density):
        def one(k):
            js = span(k, W)
            scaled[:, js] = (values[k] / density[:, js]).astype(BF16)

        loop(SIDE, one)

    scale(v1, density1)
    product_send(me, scaled, kern, part1, arrived1, sum_send_x.at[0], recv_x.at[0])

    log_pass(earlier2, later2, log2, stat_row)
    peaks2[me.row] = stat_row[...]
    stat_send(me, peaks2, stat_send_sem.at[2], recv_stat.at[2])
    sum_send(me, arrived1, sums1, final1, sum_send_z.at[0], recv_x.at[0], recv_z.at[0])
    value_next = jnp.maximum(pay_next[...].astype(F32), sum_finish(final1, recv_z.at[0]))
    out_next[...] = value_next
    own_v[1] = value_next
    v2[me.row] = value_next
    row_send(me, own_v.at[1], v2, *g(5))

    stat_finish(peaks2, recv_stat.at[2], peak, jnp.maximum)
    exp_pass(log2, kern, peak, stat_row)
    dens2[me.row] = stat_row[...]
    stat_send(me, dens2, stat_send_sem.at[3], recv_stat.at[3])
    row_relay(me, v2, *g(5))
    row_finish(me, v2, recv_gather.at[5])
    stat_finish(dens2, recv_stat.at[3], density2, jnp.add)
    scale(v2, density2)
    product_send(me, scaled, kern, part2, arrived2, sum_send_x.at[1], recv_x.at[1])
    sum_send(me, arrived2, sums2, final2, sum_send_z.at[1], recv_x.at[1], recv_z.at[1])
    out_now[...] = jnp.maximum(pay_now[...].astype(F32), sum_finish(final2, recv_z.at[1]))

    for k, buf in ((0, x1), (1, y1), (2, x2), (3, y2), (4, v1), (5, v2)):
        wait_for(buf.at[pl.ds(0, SIDE - 1)], gather_send.at[k])
    for k, buf in ((0, peaks1), (1, dens1), (2, peaks2), (3, dens2)):
        wait_for(buf.at[pl.ds(0, SIDE - 1)], stat_send_sem.at[k])
    for k, part, final in ((0, part1, final1), (1, part2, final2)):
        wait_for(part.at[pl.ds(0, QUAD * (QUAD - 1))], sum_send_x.at[k])
        wait_for(final.at[pl.ds(0, QUAD - 1)], sum_send_z.at[k])


def per_device(states_now, states_next, states_last, payoff_now, payoff_next, payoff_last):
    factors, width = states_now.shape
    swaps = payoff_now.shape[0]
    points = SIDE * width
    states = pltpu.VMEM((SIDE, factors, width), F32)
    values = pltpu.VMEM((SIDE, swaps, width), F32)
    stats = pltpu.VMEM((SIDE, 1, points), F32)
    line = pltpu.VMEM((1, points), F32)
    quad = pltpu.VMEM((QUAD, swaps, width), F32)
    square = pltpu.VMEM((QUAD, QUAD, swaps, width), F32)
    sums = [values, square, quad, quad]
    dma = pltpu.SemaphoreType.DMA
    vmem = pl.BlockSpec(memory_space=pltpu.VMEM)
    out = jax.ShapeDtypeStruct((swaps, width), F32)
    return pl.pallas_call(
        kernel_body,
        out_shape=(out, out),
        in_specs=[vmem] * 6,
        out_specs=(vmem, vmem),
        scratch_shapes=[states] * 4
        + [values, values, pltpu.VMEM((2, swaps, width), F32)]
        + [pltpu.VMEM((points, 256), BF16), pltpu.VMEM((256, points), BF16)] * 2
        + [pltpu.VMEM((points, points), F32)] * 2
        + [pltpu.VMEM((points, points), BF16), pltpu.VMEM((swaps, points), BF16)]
        + [stats] * 4
        + [line] * 4
        + sums * 2
        + [dma((4,)), dma((6,)), dma((4,)), dma((2,)), dma((2,))]
        + [dma((6, SIDE)), dma((4,)), dma((2, QUAD)), dma((2,))],
        compiler_params=pltpu.CompilerParams(
            collective_id=0, has_side_effects=True, vmem_limit_bytes=60 * 2**20
        ),
    )(states_now, states_next, states_last, payoff_now, payoff_next, payoff_last)


def solution(mesh):
    early, late = P(None, ("row", "col")), P(None, ("col", "row"))
    return jax.shard_map(
        per_device,
        mesh=mesh,
        in_specs=(late, early, late, late, early, late),
        out_specs=(early, late),
        check_vma=False,
    )
```

```python
import jax
import jax.numpy as jnp
from jax import lax
from jax.experimental import pallas as pl
from jax.experimental.pallas import tpu as pltpu
from jax.sharding import PartitionSpec as P

F32, BF16 = jnp.float32, jnp.bfloat16
W = 128
SIDE = 16
QUAD = 4
HALVES = 2
HALF = 8
MESH = pl.DeviceIdType.MESH


def span(block, width):
    return pl.ds(pl.multiple_of(block * width, width), width)


def loop(count, body):
    def step(k, carry):
        body(k)
        return carry

    lax.fori_loop(0, count, step, 0)


def split3(v):
    high = v.astype(BF16).astype(F32)
    rest = v - high
    mid = rest.astype(BF16).astype(F32)
    return high, mid, rest - mid


def operand(block, earlier):
    high, mid, low = split3(block)
    norm = split3(-0.5 * jnp.sum(block * block, axis=0, keepdims=True))
    row = lax.broadcasted_iota(jnp.int32, (8, block.shape[1]), 0)
    extra = jnp.where(row < 6, 1.0, 0.0)
    for k in range(3):
        extra = jnp.where(row == (k if earlier else k + 3), norm[k], extra)
    pieces = (high, high, mid, mid, high, low) if earlier else (high, mid, high, mid, low, high)
    return jnp.concatenate(pieces + (extra, jnp.zeros_like(extra)), axis=0)


def build_later(states, later, k):
    later[:, span(k, W)] = operand(states[k], False).astype(BF16)


def build_earlier(states, earlier, k):
    earlier[span(k, W), :] = operand(states[k], True).T.astype(BF16)


def log_pass(earlier, later, log_kernel, stat, half):
    rows, cols = 256, 256
    blocks = log_kernel.shape[1] // cols // HALVES

    def col(jc):
        js = span(half * blocks + jc, cols)

        def row(ic, top):
            i = span(ic, rows)
            tile = jnp.dot(earlier[i, :], later[:, js], preferred_element_type=F32)
            log_kernel[i, js] = tile
            return jnp.maximum(top, jnp.max(tile.reshape(rows // 8, 8, cols), axis=0))

        count = log_kernel.shape[0] // rows
        top = lax.fori_loop(0, count, row, jnp.full((8, cols), -jnp.inf, F32), unroll=True)
        stat[:, span(jc, cols)] = jnp.max(top, axis=0, keepdims=True)

    loop(blocks, col)


def exp_pass(log_kernel, kernel, peak, stat, half):
    rows, cols = 64, 256
    blocks = log_kernel.shape[1] // cols // HALVES

    def col(jc):
        js = span(half * blocks + jc, cols)
        top = jnp.broadcast_to(peak[half, :, span(jc, cols)], (8, cols))

        def row(ic, total):
            i = span(ic, rows)
            tile = jnp.exp(log_kernel[i, js].reshape(rows // 8, 8, cols) - top[None])
            kernel[i, js] = tile.reshape(rows, cols).astype(BF16)
            return total + jnp.sum(tile, axis=0)

        count = log_kernel.shape[0] // rows
        total = lax.fori_loop(0, count, row, jnp.zeros((8, cols), F32), unroll=4)
        stat[:, span(jc, cols)] = jnp.sum(total, axis=0, keepdims=True)

    loop(blocks, col)


def scale(values, density, scaled):
    blocks = SIDE // HALVES

    def one(k):
        below = density[k // blocks, :, span(k % blocks, W)]
        scaled[:, span(k, W)] = (values[k] / below).astype(BF16)

    loop(SIDE, one)


def remote(src, dst, send, recv, row, col):
    return pltpu.make_async_remote_copy(
        src_ref=src, dst_ref=dst, send_sem=send, recv_sem=recv, device_id=(row, col), device_id_type=MESH
    )


def wait_for(ref, sem):
    pltpu.make_async_copy(ref, ref, sem).wait()


class Place:
    def __init__(self):
        self.row, self.col = lax.axis_index("row"), lax.axis_index("col")
        self.chip, self.core = self.row // 2, self.row % 2
        self.z, self.x = self.col // QUAD, self.col % QUAD
        self.twin = self.chip * 2 + 1 - self.core

    def on_core(self, k):
        return ((self.chip + k) % HALF) * 2 + self.core

    def along_z(self, k):
        return ((self.z + k) % QUAD) * QUAD + self.x

    def along_x(self, k):
        return self.z * QUAD + (self.x + k) % QUAD


def row_send(me, own, buf, send, recv):
    def one(k):
        remote(own, buf.at[me.row], send, recv.at[me.row], me.on_core(k + 1), me.col).start()

    loop(HALF - 1, one)
    remote(own, buf.at[me.row], send, recv.at[me.row], me.twin, me.col).start()


def row_relay(me, buf, send, recv, then=None):
    def one(k):
        slot = me.on_core(HALF - 1 - k)
        wait_for(buf.at[slot], recv.at[slot])
        remote(buf.at[slot], buf.at[slot], send, recv.at[slot], me.twin, me.col).start()
        if then:
            then(slot)

    loop(HALF - 1, one)


def row_finish(me, buf, recv, then=None):
    def one(k):
        slot = ((me.chip + HALF - k) % HALF) * 2 + 1 - me.core
        wait_for(buf.at[slot], recv.at[slot])
        if then:
            then(slot)

    loop(HALF, one)


def col_send(me, own, buf, send, recv):
    def one(k):
        remote(own, buf.at[me.col], send, recv.at[me.col], me.row, me.along_z(k + 1)).start()

    loop(QUAD - 1, one)

    def two(k):
        remote(own, buf.at[me.col], send, recv.at[me.col], me.row, me.along_x(k + 1)).start()

    loop(QUAD - 1, two)


def col_relay(me, buf, send, recv, then=None):
    def one(k):
        slot = me.along_z(QUAD - 1 - k)
        wait_for(buf.at[slot], recv.at[slot])

        def two(q):
            remote(buf.at[slot], buf.at[slot], send, recv.at[slot], me.row, me.along_x(q + 1)).start()

        loop(QUAD - 1, two)
        if then:
            then(slot)

    loop(QUAD - 1, one)


def col_finish(me, buf, recv, then=None):
    def one(k):
        def two(q):
            slot = ((me.z + QUAD - k) % QUAD) * QUAD + (me.x + q + 1) % QUAD
            wait_for(buf.at[slot], recv.at[slot])
            if then:
                then(slot)

        loop(QUAD - 1, two)

    loop(QUAD, one)


def stat_send(me, stat, buf, send, recv):
    buf[me.row] = stat[...]
    own = buf.at[me.row]

    def one(k):
        remote(own, own, send, recv, (me.row + k + 1) % SIDE, me.col).start()

    loop(SIDE - 1, one)


def stat_finish(buf, recv, out, half, combine):
    wait_for(buf.at[pl.ds(0, SIDE - 1)], recv)
    total = buf[0]
    for k in range(1, SIDE):
        total = combine(total, buf[k])
    out[half] = total


def product_send(me, scaled, kernel, part, arrived, send, recv):
    def zs(k):
        z = (me.z + k + 1) % QUAD
        rows = kernel[span(z, QUAD * W), :]
        product = lax.dot_general(scaled[...], rows, (((1,), (1,)), ((), ())), preferred_element_type=F32)
        for x in range(QUAD):
            part[z, x] = product[:, x * W : (x + 1) * W]

        def away(q):
            x = (me.x + q + 1) % QUAD
            remote(part.at[z, x], arrived.at[z, me.x], send, recv.at[z], me.row, me.z * QUAD + x).start()

        loop(QUAD - 1, away)
        arrived[z, me.x] = part[z, me.x]

    loop(QUAD, zs)


def sum_send(me, arrived, sums, final, send, recv_x, recv_z, first, count):
    def one(k):
        z = (me.z + first + k + 1) % QUAD
        wait_for(arrived.at[z, pl.ds(0, QUAD - 1)], recv_x.at[z])
        sums[z] = arrived[z, 0] + arrived[z, 1] + arrived[z, 2] + arrived[z, 3]
        remote(sums.at[z], final.at[me.z], send, recv_z, me.row, z * QUAD + me.x).start()

    loop(count, one)


def sum_own(me, arrived, final, recv_x):
    wait_for(arrived.at[me.z, pl.ds(0, QUAD - 1)], recv_x.at[me.z])
    final[me.z] = arrived[me.z, 0] + arrived[me.z, 1] + arrived[me.z, 2] + arrived[me.z, 3]


def sum_finish(final, recv_z):
    wait_for(final.at[pl.ds(0, QUAD - 1)], recv_z)
    return final[0] + final[1] + final[2] + final[3]


def kernel_body(
    now_ref, next_ref, last_ref, pay_next_ref, pay_last_ref, out_next, out_now,
    x1, y1, x2, y2, v1, v2, own_v, pay_next, pay_last,
    earlier1, later1, earlier2, later2, log1, log2, kern, scaled,
    peaks1, dens1, peaks2, dens2, peak, density1, density2, stat,
    part1, arrived1, sums1, final1, part2, arrived2, sums2, final2,
    own_sem, gather_send, stat_sent, sum_sent_x, sum_sent_z,
    recv_gather, recv_stat, recv_x, recv_z,
):
    me = Place()

    barrier = pltpu.get_barrier_semaphore()

    def greet_col(k):
        pl.semaphore_signal(barrier, inc=1, device_id=(me.row, me.along_z(k + 1)), device_id_type=MESH)
        pl.semaphore_signal(barrier, inc=1, device_id=(me.row, me.along_x(k + 1)), device_id_type=MESH)

    loop(QUAD - 1, greet_col)

    def greet_row(k):
        pl.semaphore_signal(barrier, inc=1, device_id=((me.row + k + 1) % SIDE, me.col), device_id_type=MESH)

    loop(SIDE - 1, greet_row)

    own = [
        pltpu.make_async_copy(src, dst, own_sem.at[k])
        for k, (src, dst) in enumerate(
            (
                (next_ref, x1.at[me.col]),
                (last_ref, y1.at[me.row]),
                (now_ref, x2.at[me.col]),
                (next_ref, y2.at[me.row]),
                (pay_next_ref, pay_next),
                (pay_last_ref, pay_last),
            )
        )
    ]
    for copy in own:
        copy.start()
    for copy in own:
        copy.wait()
    own_v[0] = pay_last[...].astype(F32)
    v1[me.row] = own_v[0]
    build_earlier(x1, earlier1, me.col)
    build_later(y1, later1, me.row)
    build_earlier(x2, earlier2, me.col)
    build_later(y2, later2, me.row)
    pl.semaphore_wait(barrier, SIDE - 1 + 2 * (QUAD - 1))

    g = lambda k: (gather_send.at[k], recv_gather.at[k])
    add_x1 = lambda k: build_earlier(x1, earlier1, k)
    add_y1 = lambda k: build_later(y1, later1, k)
    add_x2 = lambda k: build_earlier(x2, earlier2, k)
    add_y2 = lambda k: build_later(y2, later2, k)

    col_send(me, x1.at[me.col], x1, *g(0))
    row_send(me, y1.at[me.row], y1, *g(1))
    row_relay(me, y1, *g(1), add_y1)
    col_relay(me, x1, *g(0), add_x1)
    row_send(me, own_v.at[0], v1, *g(4))
    row_send(me, y2.at[me.row], y2, *g(3))
    col_send(me, x2.at[me.col], x2, *g(2))
    row_finish(me, y1, recv_gather.at[1], add_y1)
    col_finish(me, x1, recv_gather.at[0], add_x1)

    log_pass(earlier1, later1, log1, stat.at[0], 0)
    stat_send(me, stat.at[0], peaks1.at[0], stat_sent.at[0, 0], recv_stat.at[0, 0])
    row_relay(me, v1, *g(4))
    row_relay(me, y2, *g(3), add_y2)
    log_pass(earlier1, later1, log1, stat.at[0], 1)
    stat_send(me, stat.at[0], peaks1.at[1], stat_sent.at[0, 1], recv_stat.at[0, 1])
    col_relay(me, x2, *g(2), add_x2)
    row_finish(me, y2, recv_gather.at[3], add_y2)

    for half in range(HALVES):
        stat_finish(peaks1.at[half], recv_stat.at[0, half], peak, half, jnp.maximum)
        exp_pass(log1, kern, peak, stat.at[0], half)
        stat_send(me, stat.at[0], dens1.at[half], stat_sent.at[1, half], recv_stat.at[1, half])

    col_finish(me, x2, recv_gather.at[2], add_x2)
    row_finish(me, v1, recv_gather.at[4])
    for half in range(HALVES):
        log_pass(earlier2, later2, log2, stat.at[0], half)
        stat_send(me, stat.at[0], peaks2.at[half], stat_sent.at[2, half], recv_stat.at[2, half])

    for half in range(HALVES):
        stat_finish(dens1.at[half], recv_stat.at[1, half], density1, half, jnp.add)
    scale(v1, density1, scaled)
    product_send(me, scaled, kern, part1, arrived1, sum_sent_x.at[0], recv_x.at[0])

    sums = (arrived1, sums1, final1, sum_sent_z.at[0], recv_x.at[0], recv_z.at[0])
    for half in range(HALVES):
        stat_finish(peaks2.at[half], recv_stat.at[2, half], peak, half, jnp.maximum)
        exp_pass(log2, kern, peak, stat.at[0], half)
        stat_send(me, stat.at[0], dens2.at[half], stat_sent.at[3, half], recv_stat.at[3, half])
        if half == 0:
            sum_send(me, *sums, 0, QUAD - 1)
    sum_own(me, arrived1, final1, recv_x.at[0])
    held = sum_finish(final1, recv_z.at[0])
    out_next[...] = held
    value_next = jnp.maximum(pay_next[...].astype(F32), held)
    own_v[1] = value_next
    v2[me.row] = value_next
    row_send(me, own_v.at[1], v2, *g(5))

    for half in range(HALVES):
        stat_finish(dens2.at[half], recv_stat.at[3, half], density2, half, jnp.add)
    row_relay(me, v2, *g(5))
    row_finish(me, v2, recv_gather.at[5])
    scale(v2, density2, scaled)
    product_send(me, scaled, kern, part2, arrived2, sum_sent_x.at[1], recv_x.at[1])
    sum_send(me, arrived2, sums2, final2, sum_sent_z.at[1], recv_x.at[1], recv_z.at[1], 0, QUAD - 1)
    sum_own(me, arrived2, final2, recv_x.at[1])
    out_now[...] = sum_finish(final2, recv_z.at[1])

    for k, buf in ((0, x1), (1, y1), (2, x2), (3, y2), (4, v1), (5, v2)):
        wait_for(buf.at[pl.ds(0, SIDE - 1)], gather_send.at[k])
    for k, buf in ((0, peaks1), (1, dens1), (2, peaks2), (3, dens2)):
        for half in range(HALVES):
            wait_for(buf.at[half, pl.ds(0, SIDE - 1)], stat_sent.at[k, half])
    for k, part, final in ((0, part1, final1), (1, part2, final2)):
        wait_for(part.at[pl.ds(0, QUAD - 1)], sum_sent_x.at[k])
        wait_for(final.at[pl.ds(0, QUAD - 1)], sum_sent_z.at[k])


def per_device(states_now, states_next, states_last, payoff_now, payoff_next, payoff_last):
    factors, width = states_now.shape
    swaps = payoff_now.shape[0]
    points = SIDE * width
    states = pltpu.VMEM((SIDE, factors, width), F32)
    values = pltpu.VMEM((SIDE, swaps, width), F32)
    stats = pltpu.VMEM((HALVES, SIDE, 1, points // HALVES), F32)
    line = pltpu.VMEM((HALVES, 1, points // HALVES), F32)
    quad = pltpu.VMEM((QUAD, swaps, width), F32)
    square = pltpu.VMEM((QUAD, QUAD, swaps, width), F32)
    payoff = pltpu.VMEM((swaps, width), BF16)
    dma = pltpu.SemaphoreType.DMA
    vmem = pl.BlockSpec(memory_space=pltpu.VMEM)
    out = jax.ShapeDtypeStruct((swaps, width), F32)
    held_next, held_now = pl.pallas_call(
        kernel_body,
        out_shape=(out, out),
        in_specs=[pl.BlockSpec(memory_space=pl.ANY)] * 5,
        out_specs=(vmem, vmem),
        scratch_shapes=[states] * 4
        + [values, values, pltpu.VMEM((2, swaps, width), F32), payoff, payoff]
        + [pltpu.VMEM((points, 256), BF16), pltpu.VMEM((256, points), BF16)] * 2
        + [pltpu.VMEM((points, points), F32)] * 2
        + [pltpu.VMEM((points, points), BF16), pltpu.VMEM((swaps, points), BF16)]
        + [stats] * 4
        + [line] * 4
        + [square, square, quad, quad] * 2
        + [dma((6,)), dma((6,)), dma((4, HALVES)), dma((2,)), dma((2,))]
        + [dma((6, SIDE)), dma((4, HALVES)), dma((2, QUAD)), dma((2,))],
        compiler_params=pltpu.CompilerParams(
            collective_id=0, has_side_effects=True, vmem_limit_bytes=60 * 2**20
        ),
    )(states_now, states_next, states_last, payoff_next, payoff_last)
    return jnp.maximum(payoff_next.astype(F32), held_next), jnp.maximum(payoff_now.astype(F32), held_now)


def solution(mesh):
    early, late = P(None, ("row", "col")), P(None, ("col", "row"))
    return jax.shard_map(
        per_device,
        mesh=mesh,
        in_specs=(late, early, late, late, early, late),
        out_specs=(early, late),
        check_vma=False,
    )
```

```python
import jax
import jax.numpy as jnp
from jax import lax
from jax.experimental import pallas as pl
from jax.experimental.pallas import tpu as pltpu
from jax.sharding import PartitionSpec as P

F32, BF16 = jnp.float32, jnp.bfloat16
W = 128
SIDE = 16
QUAD = 4
HALVES = 2
HALF = 8
MESH = pl.DeviceIdType.MESH


def span(block, width):
    return pl.ds(pl.multiple_of(block * width, width), width)


def loop(count, body):
    def step(k, carry):
        body(k)
        return carry

    lax.fori_loop(0, count, step, 0)


def split3(v):
    high = v.astype(BF16).astype(F32)
    rest = v - high
    mid = rest.astype(BF16).astype(F32)
    return high, mid, rest - mid


def operand(block, earlier):
    high, mid, low = split3(block)
    norm = split3(-0.5 * jnp.sum(block * block, axis=0, keepdims=True))
    row = lax.broadcasted_iota(jnp.int32, (8, block.shape[1]), 0)
    extra = jnp.where(row < 6, 1.0, 0.0)
    for k in range(3):
        extra = jnp.where(row == (k if earlier else k + 3), norm[k], extra)
    pieces = (high, high, mid, mid, high, low) if earlier else (high, mid, high, mid, low, high)
    return jnp.concatenate(pieces + (extra, jnp.zeros_like(extra)), axis=0)


def build_later(states, later, k):
    later[:, span(k, W)] = operand(states[k], False).astype(BF16)


def build_earlier(states, earlier, k):
    earlier[span(k, W), :] = operand(states[k], True).T.astype(BF16)


def log_tiles(earlier, later, log_kernel, top, first_row, rows, first_col, cols):
    tile_rows, tile_cols = 256, 256
    for jc in range(cols // tile_cols):
        js = pl.ds(pl.multiple_of(first_col + jc * tile_cols, tile_cols), tile_cols)
        highest = top[:, js]
        for ic in range(rows // tile_rows):
            i = pl.ds(pl.multiple_of(first_row + ic * tile_rows, tile_rows), tile_rows)
            tile = jnp.dot(earlier[i, :], later[:, js], preferred_element_type=F32)
            log_kernel[i, js] = tile
            highest = jnp.maximum(highest, jnp.max(tile.reshape(tile_rows // 8, 8, tile_cols), axis=0))
        top[:, js] = highest


def exp_pass(log_kernel, kernel, peak, stat, half):
    rows, cols = 64, 256
    blocks = log_kernel.shape[1] // cols // HALVES

    def col(jc):
        js = span(half * blocks + jc, cols)
        top = jnp.broadcast_to(peak[half, :, span(jc, cols)], (8, cols))

        def row(ic, total):
            i = span(ic, rows)
            tile = jnp.exp(log_kernel[i, js].reshape(rows // 8, 8, cols) - top[None])
            kernel[i, js] = tile.reshape(rows, cols).astype(BF16)
            return total + jnp.sum(tile, axis=0)

        count = log_kernel.shape[0] // rows
        total = lax.fori_loop(0, count, row, jnp.zeros((8, cols), F32), unroll=True)
        stat[:, span(jc, cols)] = jnp.sum(total, axis=0, keepdims=True)

    loop(blocks, col)


def scale(values, density, scaled):
    blocks = SIDE // HALVES

    def one(k):
        below = density[k // blocks, :, span(k % blocks, W)]
        scaled[:, span(k, W)] = (values[k] / below).astype(BF16)

    loop(SIDE, one)


def remote(src, dst, send, recv, row, col):
    return pltpu.make_async_remote_copy(
        src_ref=src, dst_ref=dst, send_sem=send, recv_sem=recv, device_id=(row, col), device_id_type=MESH
    )


def wait_for(ref, sem):
    pltpu.make_async_copy(ref, ref, sem).wait()


class Place:
    def __init__(self):
        self.row, self.col = lax.axis_index("row"), lax.axis_index("col")
        self.chip, self.core = self.row // 2, self.row % 2
        self.low, self.y = self.chip // QUAD, self.chip % QUAD
        self.z, self.x = self.col // QUAD, self.col % QUAD
        self.twin = self.chip * 2 + 1 - self.core

    def on_core(self, k, other=0):
        core = 1 - self.core if other else self.core
        return (((self.low + k // QUAD) % 2) * QUAD + (self.y + near(k % QUAD)) % QUAD) * 2 + core

    def along_z(self, k):
        return ((self.z + k) % QUAD) * QUAD + self.x

    def along_x(self, k):
        return self.z * QUAD + (self.x + k) % QUAD


def near(k):
    return k + k // 2 - 2 * (k // 3)


def far(k):
    return 2 - k + 3 * (k // 2) - 2 * (k // 3)


def row_send(me, own, buf, send, recv):
    def one(k):
        remote(own, buf.at[me.row], send, recv.at[me.row], me.on_core(HALF - 1 - k), me.col).start()

    loop(HALF - 1, one)
    remote(own, buf.at[me.row], send, recv.at[me.row], me.twin, me.col).start()


def row_relay(me, buf, send, recv):
    def one(k):
        slot = me.on_core(k + 1)
        wait_for(buf.at[slot], recv.at[slot])
        remote(buf.at[slot], buf.at[slot], send, recv.at[slot], me.twin, me.col).start()

    loop(HALF - 1, one)


def row_finish(me, buf, recv, then):
    def one(k):
        then(me.on_core(k))
        slot = me.on_core(k, other=1)
        wait_for(buf.at[slot], recv.at[slot])
        then(slot)

    loop(HALF, one)


def col_send(me, own, buf, send, recv):
    def along_z(k):
        remote(own, buf.at[me.col], send, recv.at[me.col], me.row, me.along_z(far(k))).start()

    def along_x(k):
        remote(own, buf.at[me.col], send, recv.at[me.col], me.row, me.along_x(far(k))).start()

    loop(QUAD - 1, along_z)
    loop(QUAD - 1, along_x)


def col_relay(me, buf, send, recv):
    def one(k):
        slot = me.along_z(near(k + 1))
        wait_for(buf.at[slot], recv.at[slot])

        def two(q):
            remote(buf.at[slot], buf.at[slot], send, recv.at[slot], me.row, me.along_x(far(q))).start()

        loop(QUAD - 1, two)

    loop(QUAD - 1, one)


def col_finish(me, buf, recv, k, then):
    group = (me.z + k) % QUAD
    then(group * QUAD + me.x)

    def one(q):
        slot = group * QUAD + (me.x + near(q + 1)) % QUAD
        wait_for(buf.at[slot], recv.at[slot])
        then(slot)

    loop(QUAD - 1, one)
    return group


def stat_send(me, stat, buf, send, recv):
    buf[me.row] = stat[...]
    own = buf.at[me.row]

    def one(k):
        remote(own, own, send, recv, (me.row + k + 1) % SIDE, me.col).start()

    loop(SIDE - 1, one)


def stat_finish(buf, recv, out, half, combine):
    wait_for(buf.at[pl.ds(0, SIDE - 1)], recv)
    total = buf[0]
    for k in range(1, SIDE):
        total = combine(total, buf[k])
    out[half] = total


def product_send(me, scaled, kernel, part, arrived, send, recv):
    def zs(k):
        z = (me.z + far(k)) % QUAD
        rows = kernel[span(z, QUAD * W), :]
        product = lax.dot_general(scaled[...], rows, (((1,), (1,)), ((), ())), preferred_element_type=F32)
        for x in range(QUAD):
            part[z, x] = product[:, x * W : (x + 1) * W]

        def away(q):
            x = (me.x + far(q)) % QUAD
            remote(part.at[z, x], arrived.at[z, me.x], send, recv.at[z], me.row, me.z * QUAD + x).start()

        loop(QUAD - 1, away)
        arrived[z, me.x] = part[z, me.x]

    loop(QUAD, zs)


def sum_send(me, arrived, sums, final, send, recv_x, recv_z):
    def one(k):
        z = (me.z + far(k)) % QUAD
        wait_for(arrived.at[z, pl.ds(0, QUAD - 1)], recv_x.at[z])
        sums[z] = arrived[z, 0] + arrived[z, 1] + arrived[z, 2] + arrived[z, 3]
        remote(sums.at[z], final.at[me.z], send, recv_z, me.row, z * QUAD + me.x).start()

    loop(QUAD - 1, one)


def sum_own(me, arrived, final, recv_x):
    wait_for(arrived.at[me.z, pl.ds(0, QUAD - 1)], recv_x.at[me.z])
    final[me.z] = arrived[me.z, 0] + arrived[me.z, 1] + arrived[me.z, 2] + arrived[me.z, 3]


def sum_finish(final, recv_z):
    wait_for(final.at[pl.ds(0, QUAD - 1)], recv_z)
    return final[0] + final[1] + final[2] + final[3]


def kernel_body(
    now_ref, next_ref, last_ref, pay_next_ref, pay_last_ref, out_next, out_now,
    x1, y1, x2, y2, v1, v2, own_v, pay_next, pay_last,
    earlier1, later1, earlier2, later2, log1, log2, kern, scaled,
    peaks1, dens1, peaks2, dens2, peak, density1, density2, stat, top,
    part1, arrived1, sums1, final1, part2, arrived2, sums2, final2,
    own_sem, gather_send, stat_sent, sum_sent_x, sum_sent_z,
    recv_gather, recv_stat, recv_x, recv_z,
):
    me = Place()
    points, width = log1.shape[1], stat.shape[2]

    barrier = pltpu.get_barrier_semaphore()

    def greet_col(k):
        pl.semaphore_signal(barrier, inc=1, device_id=(me.row, me.along_z(k + 1)), device_id_type=MESH)
        pl.semaphore_signal(barrier, inc=1, device_id=(me.row, me.along_x(k + 1)), device_id_type=MESH)

    loop(QUAD - 1, greet_col)

    def greet_row(k):
        pl.semaphore_signal(barrier, inc=1, device_id=((me.row + k + 1) % SIDE, me.col), device_id_type=MESH)

    loop(SIDE - 1, greet_row)

    own = [
        pltpu.make_async_copy(src, dst, own_sem.at[k])
        for k, (src, dst) in enumerate(
            (
                (next_ref, x1.at[me.col]),
                (last_ref, y1.at[me.row]),
                (now_ref, x2.at[me.col]),
                (next_ref, y2.at[me.row]),
                (pay_next_ref, pay_next),
                (pay_last_ref, pay_last),
            )
        )
    ]
    for copy in own:
        copy.start()
    for copy in own:
        copy.wait()
    own_v[0] = pay_last[...].astype(F32)
    v1[me.row] = own_v[0]
    top[...] = jnp.full_like(top, -jnp.inf)
    pl.semaphore_wait(barrier, SIDE - 1 + 2 * (QUAD - 1))

    g = lambda k: (gather_send.at[k], recv_gather.at[k])
    add_x1 = lambda k: build_earlier(x1, earlier1, k)
    add_y1 = lambda k: build_later(y1, later1, k)
    add_x2 = lambda k: build_earlier(x2, earlier2, k)
    add_y2 = lambda k: build_later(y2, later2, k)

    col_send(me, x1.at[me.col], x1, *g(0))
    row_send(me, y1.at[me.row], y1, *g(1))
    row_relay(me, y1, *g(1))
    col_relay(me, x1, *g(0))
    row_send(me, own_v.at[0], v1, *g(4))
    row_send(me, y2.at[me.row], y2, *g(3))
    col_send(me, x2.at[me.col], x2, *g(2))
    row_finish(me, y1, recv_gather.at[1], add_y1)

    def group_in(k):
        group = col_finish(me, x1, recv_gather.at[0], near(k), add_x1)
        log_tiles(earlier1, later1, log1, top, group * QUAD * W, QUAD * W, 0, points)

    def stat_out(k, buf, half):
        stat_send(me, stat.at[half], buf.at[half], stat_sent.at[k, half], recv_stat.at[k, half])

    def peaks_out(half):
        log_tiles(earlier1, later1, log1, top, last * QUAD * W, QUAD * W, half * width, width)
        stat[half] = jnp.max(top[:, span(half, width)], axis=0, keepdims=True)
        stat_out(0, peaks1, half)

    loop(QUAD - 1, group_in)
    last = col_finish(me, x1, recv_gather.at[0], 2, add_x1)
    loop(HALVES, peaks_out)
    top[...] = jnp.full_like(top, -jnp.inf)

    row_relay(me, v1, *g(4))
    row_relay(me, y2, *g(3))
    col_relay(me, x2, *g(2))
    row_finish(me, y2, recv_gather.at[3], add_y2)

    def dens_out(half):
        stat_finish(peaks1.at[half], recv_stat.at[0, half], peak, half, jnp.maximum)
        exp_pass(log1, kern, peak, stat.at[half], half)
        stat_out(1, dens1, half)

    loop(HALVES, dens_out)

    loop(QUAD, lambda k: (col_finish(me, x2, recv_gather.at[2], near(k), add_x2), None)[1])
    row_finish(me, v1, recv_gather.at[4], lambda k: None)

    def peaks_out_2(half):
        part = width // 2
        loop(2, lambda k: log_tiles(earlier2, later2, log2, top, 0, points, half * width + k * part, part))
        stat[half] = jnp.max(top[:, span(half, width)], axis=0, keepdims=True)
        stat_out(2, peaks2, half)

    loop(HALVES, peaks_out_2)
    loop(HALVES, lambda half: stat_finish(dens1.at[half], recv_stat.at[1, half], density1, half, jnp.add))
    scale(v1, density1, scaled)
    product_send(me, scaled, kern, part1, arrived1, sum_sent_x.at[0], recv_x.at[0])

    def dens_out_2(half):
        stat_finish(peaks2.at[half], recv_stat.at[2, half], peak, half, jnp.maximum)
        exp_pass(log2, kern, peak, stat.at[half], half)
        stat_out(3, dens2, half)

    dens_out_2(0)
    sum_send(me, arrived1, sums1, final1, sum_sent_z.at[0], recv_x.at[0], recv_z.at[0])
    dens_out_2(1)
    sum_own(me, arrived1, final1, recv_x.at[0])
    held = sum_finish(final1, recv_z.at[0])
    out_next[...] = held
    value_next = jnp.maximum(pay_next[...].astype(F32), held)
    own_v[1] = value_next
    v2[me.row] = value_next
    row_send(me, own_v.at[1], v2, *g(5))

    loop(HALVES, lambda half: stat_finish(dens2.at[half], recv_stat.at[3, half], density2, half, jnp.add))
    row_relay(me, v2, *g(5))
    row_finish(me, v2, recv_gather.at[5], lambda k: None)
    scale(v2, density2, scaled)
    product_send(me, scaled, kern, part2, arrived2, sum_sent_x.at[1], recv_x.at[1])
    sum_send(me, arrived2, sums2, final2, sum_sent_z.at[1], recv_x.at[1], recv_z.at[1])
    sum_own(me, arrived2, final2, recv_x.at[1])
    out_now[...] = sum_finish(final2, recv_z.at[1])

    for k, buf in ((0, x1), (1, y1), (2, x2), (3, y2), (4, v1), (5, v2)):
        wait_for(buf.at[pl.ds(0, SIDE - 1)], gather_send.at[k])
    for k, buf in ((0, peaks1), (1, dens1), (2, peaks2), (3, dens2)):
        for half in range(HALVES):
            wait_for(buf.at[half, pl.ds(0, SIDE - 1)], stat_sent.at[k, half])
    for k, part, final in ((0, part1, final1), (1, part2, final2)):
        wait_for(part.at[pl.ds(0, QUAD - 1)], sum_sent_x.at[k])
        wait_for(final.at[pl.ds(0, QUAD - 1)], sum_sent_z.at[k])


def per_device(states_now, states_next, states_last, payoff_now, payoff_next, payoff_last):
    factors, width = states_now.shape
    swaps = payoff_now.shape[0]
    points = SIDE * width
    states = pltpu.VMEM((SIDE, factors, width), F32)
    values = pltpu.VMEM((SIDE, swaps, width), F32)
    stats = pltpu.VMEM((HALVES, SIDE, 1, points // HALVES), F32)
    line = pltpu.VMEM((HALVES, 1, points // HALVES), F32)
    quad = pltpu.VMEM((QUAD, swaps, width), F32)
    square = pltpu.VMEM((QUAD, QUAD, swaps, width), F32)
    payoff = pltpu.VMEM((swaps, width), BF16)
    dma = pltpu.SemaphoreType.DMA
    vmem = pl.BlockSpec(memory_space=pltpu.VMEM)
    out = jax.ShapeDtypeStruct((swaps, width), F32)
    held_next, held_now = pl.pallas_call(
        kernel_body,
        out_shape=(out, out),
        in_specs=[pl.BlockSpec(memory_space=pl.ANY)] * 5,
        out_specs=(vmem, vmem),
        scratch_shapes=[states] * 4
        + [values, values, pltpu.VMEM((2, swaps, width), F32), payoff, payoff]
        + [pltpu.VMEM((points, 256), BF16), pltpu.VMEM((256, points), BF16)] * 2
        + [pltpu.VMEM((points, points), F32)] * 2
        + [pltpu.VMEM((points, points), BF16), pltpu.VMEM((swaps, points), BF16)]
        + [stats] * 4
        + [line] * 4
        + [pltpu.VMEM((8, points), F32)]
        + [square, square, quad, quad] * 2
        + [dma((6,)), dma((6,)), dma((4, HALVES)), dma((2,)), dma((2,))]
        + [dma((6, SIDE)), dma((4, HALVES)), dma((2, QUAD)), dma((2,))],
        compiler_params=pltpu.CompilerParams(
            collective_id=0, has_side_effects=True, vmem_limit_bytes=60 * 2**20
        ),
    )(states_now, states_next, states_last, payoff_next, payoff_last)
    return jnp.maximum(payoff_next.astype(F32), held_next), jnp.maximum(payoff_now.astype(F32), held_now)


def solution(mesh):
    early, late = P(None, ("row", "col")), P(None, ("col", "row"))
    return jax.shard_map(
        per_device,
        mesh=mesh,
        in_specs=(late, early, late, late, early, late),
        out_specs=(early, late),
        check_vma=False,
    )
```

```python
import jax
import jax.numpy as jnp
from jax import lax
from jax.experimental import pallas as pl
from jax.experimental.pallas import tpu as pltpu
from jax.sharding import PartitionSpec as P

F32, BF16 = jnp.float32, jnp.bfloat16
W = 128
SIDE = 16
QUAD = 4
HALVES = 2
HALF = 8
MESH = pl.DeviceIdType.MESH


def span(block, width):
    return pl.ds(pl.multiple_of(block * width, width), width)


def loop(count, body):
    def step(k, carry):
        body(k)
        return carry

    lax.fori_loop(0, count, step, 0)


def split3(v):
    high = v.astype(BF16).astype(F32)
    rest = v - high
    mid = rest.astype(BF16).astype(F32)
    return high, mid, rest - mid


def operand(block, earlier):
    high, mid, low = split3(block)
    norm = split3(-0.5 * jnp.sum(block * block, axis=0, keepdims=True))
    row = lax.broadcasted_iota(jnp.int32, (8, block.shape[1]), 0)
    extra = jnp.where(row < 6, 1.0, 0.0)
    for k in range(3):
        extra = jnp.where(row == (k if earlier else k + 3), norm[k], extra)
    pieces = (high, high, mid, mid, high, low) if earlier else (high, mid, high, mid, low, high)
    return jnp.concatenate(pieces + (extra, jnp.zeros_like(extra)), axis=0)


def build_later(states, later, k):
    later[:, span(k, W)] = operand(states[k], False).astype(BF16)


def build_earlier(states, earlier, k):
    earlier[span(k, W), :] = operand(states[k], True).T.astype(BF16)


def log_tiles(earlier, later, log_kernel, top, first_row, rows, first_col, cols):
    tile_rows, tile_cols = 256, 256
    for jc in range(cols // tile_cols):
        js = pl.ds(pl.multiple_of(first_col + jc * tile_cols, tile_cols), tile_cols)
        highest = top[:, js]
        for ic in range(rows // tile_rows):
            i = pl.ds(pl.multiple_of(first_row + ic * tile_rows, tile_rows), tile_rows)
            tile = jnp.dot(earlier[i, :], later[:, js], preferred_element_type=F32)
            log_kernel[i, js] = tile
            highest = jnp.maximum(highest, jnp.max(tile.reshape(tile_rows // 8, 8, tile_cols), axis=0))
        top[:, js] = highest


def exp_pass(log_kernel, kernel, peak, stat, half):
    rows, cols = 64, 256
    blocks = log_kernel.shape[1] // cols // HALVES

    def col(jc):
        js = span(half * blocks + jc, cols)
        top = jnp.broadcast_to(peak[half, :, span(jc, cols)], (8, cols))

        def row(ic, total):
            i = span(ic, rows)
            tile = jnp.exp(log_kernel[i, js].reshape(rows // 8, 8, cols) - top[None])
            kernel[i, js] = tile.reshape(rows, cols).astype(BF16)
            return total + jnp.sum(tile, axis=0)

        count = log_kernel.shape[0] // rows
        total = lax.fori_loop(0, count, row, jnp.zeros((8, cols), F32), unroll=True)
        stat[:, span(jc, cols)] = jnp.sum(total, axis=0, keepdims=True)

    loop(blocks, col)


def scale(values, density, scaled):
    blocks = SIDE // HALVES

    def one(k):
        below = density[k // blocks, :, span(k % blocks, W)]
        scaled[:, span(k, W)] = (values[k] / below).astype(BF16)

    loop(SIDE, one)


def remote(src, dst, send, recv, row, col):
    return pltpu.make_async_remote_copy(
        src_ref=src, dst_ref=dst, send_sem=send, recv_sem=recv, device_id=(row, col), device_id_type=MESH
    )


def wait_for(ref, sem):
    pltpu.make_async_copy(ref, ref, sem).wait()


class Place:
    def __init__(self):
        self.row, self.col = lax.axis_index("row"), lax.axis_index("col")
        self.chip, self.core = self.row // 2, self.row % 2
        self.low, self.y = self.chip // QUAD, self.chip % QUAD
        self.z, self.x = self.col // QUAD, self.col % QUAD
        self.twin = self.chip * 2 + 1 - self.core

    def on_core(self, k, other=0):
        core = 1 - self.core if other else self.core
        return (((self.low + k // QUAD) % 2) * QUAD + (self.y + near(k % QUAD)) % QUAD) * 2 + core

    def along_z(self, k):
        return ((self.z + k) % QUAD) * QUAD + self.x

    def along_x(self, k):
        return self.z * QUAD + (self.x + k) % QUAD


def near(k):
    return k + k // 2 - 2 * (k // 3)


def far(k):
    return 2 - k + 3 * (k // 2) - 2 * (k // 3)


def row_send(me, own, buf, send, recv):
    def one(k):
        remote(own, buf.at[me.row], send, recv.at[me.row], me.on_core(HALF - 1 - k), me.col).start()

    loop(HALF - 1, one)
    remote(own, buf.at[me.row], send, recv.at[me.row], me.twin, me.col).start()


def row_relay(me, buf, send, recv):
    def one(k):
        slot = me.on_core(k + 1)
        wait_for(buf.at[slot], recv.at[slot])
        remote(buf.at[slot], buf.at[slot], send, recv.at[slot], me.twin, me.col).start()

    loop(HALF - 1, one)


def row_finish(me, buf, recv, then):
    def one(k):
        then(me.on_core(k))
        slot = me.on_core(k, other=1)
        wait_for(buf.at[slot], recv.at[slot])
        then(slot)

    loop(HALF, one)


def col_send(me, own, buf, send, recv):
    def along_z(k):
        remote(own, buf.at[me.col], send, recv.at[me.col], me.row, me.along_z(far(k))).start()

    def along_x(k):
        remote(own, buf.at[me.col], send, recv.at[me.col], me.row, me.along_x(far(k))).start()

    loop(QUAD - 1, along_z)
    loop(QUAD - 1, along_x)


def col_relay(me, buf, send, recv):
    def one(k):
        slot = me.along_z(near(k + 1))
        wait_for(buf.at[slot], recv.at[slot])

        def two(q):
            remote(buf.at[slot], buf.at[slot], send, recv.at[slot], me.row, me.along_x(far(q))).start()

        loop(QUAD - 1, two)

    loop(QUAD - 1, one)


def col_finish(me, buf, recv, k, then):
    group = (me.z + k) % QUAD
    then(group * QUAD + me.x)

    def one(q):
        slot = group * QUAD + (me.x + near(q + 1)) % QUAD
        wait_for(buf.at[slot], recv.at[slot])
        then(slot)

    loop(QUAD - 1, one)
    return group


def stat_send(me, stat, buf, send, recv):
    buf[me.row] = stat[...]
    own = buf.at[me.row]

    def one(k):
        remote(own, own, send, recv, (me.row + k + 1) % SIDE, me.col).start()

    loop(SIDE - 1, one)


def stat_finish(buf, recv, out, half, combine):
    wait_for(buf.at[pl.ds(0, SIDE - 1)], recv)
    total = buf[0]
    for k in range(1, SIDE):
        total = combine(total, buf[k])
    out[half] = total


def product_send(me, scaled, kernel, part, arrived, send, recv):
    def zs(k):
        z = (me.z + far(k)) % QUAD
        rows = kernel[span(z, QUAD * W), :]
        product = lax.dot_general(scaled[...], rows, (((1,), (1,)), ((), ())), preferred_element_type=F32)
        for x in range(QUAD):
            part[z, x] = product[:, x * W : (x + 1) * W]

        def away(q):
            x = (me.x + far(q)) % QUAD
            remote(part.at[z, x], arrived.at[z, me.x], send, recv.at[z], me.row, me.z * QUAD + x).start()

        loop(QUAD - 1, away)
        arrived[z, me.x] = part[z, me.x]

    loop(QUAD, zs)


def sum_send(me, arrived, sums, final, send, recv_x, recv_z):
    def one(k):
        z = (me.z + far(k)) % QUAD
        wait_for(arrived.at[z, pl.ds(0, QUAD - 1)], recv_x.at[z])
        sums[z] = arrived[z, 0] + arrived[z, 1] + arrived[z, 2] + arrived[z, 3]
        remote(sums.at[z], final.at[me.z], send, recv_z, me.row, z * QUAD + me.x).start()

    loop(QUAD - 1, one)


def sum_own(me, arrived, final, recv_x):
    wait_for(arrived.at[me.z, pl.ds(0, QUAD - 1)], recv_x.at[me.z])
    final[me.z] = arrived[me.z, 0] + arrived[me.z, 1] + arrived[me.z, 2] + arrived[me.z, 3]


def sum_finish(final, recv_z):
    wait_for(final.at[pl.ds(0, QUAD - 1)], recv_z)
    return final[0] + final[1] + final[2] + final[3]


def kernel_body(
    now_ref, next_ref, last_ref, pay_next_ref, pay_last_ref, out_next, out_now,
    x1, y1, x2, y2, v1, v2, own_v, pay_next, pay_last,
    earlier1, later1, earlier2, later2, log1, log2, kern, scaled,
    peaks1, dens1, peaks2, dens2, peak, density1, density2, stat, top,
    part1, arrived1, sums1, final1, part2, arrived2, sums2, final2,
    own_sem, gather_send, stat_sent, sum_sent_x, sum_sent_z,
    recv_gather, recv_stat, recv_x, recv_z,
):
    me = Place()
    points, width = log1.shape[1], stat.shape[2]

    barrier = pltpu.get_barrier_semaphore()

    def greet_col(k):
        pl.semaphore_signal(barrier, inc=1, device_id=(me.row, me.along_z(k + 1)), device_id_type=MESH)
        pl.semaphore_signal(barrier, inc=1, device_id=(me.row, me.along_x(k + 1)), device_id_type=MESH)

    loop(QUAD - 1, greet_col)

    def greet_row(k):
        pl.semaphore_signal(barrier, inc=1, device_id=((me.row + k + 1) % SIDE, me.col), device_id_type=MESH)

    loop(SIDE - 1, greet_row)

    own = [
        pltpu.make_async_copy(src, dst, own_sem.at[k])
        for k, (src, dst) in enumerate(
            (
                (next_ref, x1.at[me.col]),
                (last_ref, y1.at[me.row]),
                (now_ref, x2.at[me.col]),
                (next_ref, y2.at[me.row]),
                (pay_next_ref, pay_next),
                (pay_last_ref, pay_last),
            )
        )
    ]
    for copy in own:
        copy.start()
    for copy in own:
        copy.wait()
    own_v[0] = pay_last[...].astype(F32)
    v1[me.row] = own_v[0]
    top[...] = jnp.full_like(top, -jnp.inf)
    pl.semaphore_wait(barrier, SIDE - 1 + 2 * (QUAD - 1))

    g = lambda k: (gather_send.at[k], recv_gather.at[k])
    add_x1 = lambda k: build_earlier(x1, earlier1, k)
    add_y1 = lambda k: build_later(y1, later1, k)
    add_x2 = lambda k: build_earlier(x2, earlier2, k)
    add_y2 = lambda k: build_later(y2, later2, k)

    col_send(me, x1.at[me.col], x1, *g(0))
    row_send(me, y1.at[me.row], y1, *g(1))
    row_relay(me, y1, *g(1))
    col_relay(me, x1, *g(0))
    row_send(me, own_v.at[0], v1, *g(4))
    row_send(me, y2.at[me.row], y2, *g(3))
    col_send(me, x2.at[me.col], x2, *g(2))
    row_finish(me, y1, recv_gather.at[1], add_y1)

    def group_in(k):
        group = col_finish(me, x1, recv_gather.at[0], near(k), add_x1)
        log_tiles(earlier1, later1, log1, top, group * QUAD * W, QUAD * W, 0, points)

    def stat_out(k, buf, half):
        stat_send(me, stat.at[half], buf.at[half], stat_sent.at[k, half], recv_stat.at[k, half])

    def peaks_out(half):
        log_tiles(earlier1, later1, log1, top, last * QUAD * W, QUAD * W, half * width, width)
        stat[half] = jnp.max(top[:, span(half, width)], axis=0, keepdims=True)
        stat_out(0, peaks1, half)

    loop(QUAD - 1, group_in)
    last = col_finish(me, x1, recv_gather.at[0], 2, add_x1)
    loop(HALVES, peaks_out)
    top[...] = jnp.full_like(top, -jnp.inf)

    row_relay(me, v1, *g(4))
    row_relay(me, y2, *g(3))
    col_relay(me, x2, *g(2))
    row_finish(me, y2, recv_gather.at[3], add_y2)

    def dens_out(half):
        stat_finish(peaks1.at[half], recv_stat.at[0, half], peak, half, jnp.maximum)
        exp_pass(log1, kern, peak, stat.at[half], half)
        stat_out(1, dens1, half)

    loop(HALVES, dens_out)

    loop(QUAD, lambda k: (col_finish(me, x2, recv_gather.at[2], near(k), add_x2), None)[1])
    row_finish(me, v1, recv_gather.at[4], lambda k: None)

    def peaks_out_2(half):
        part = width // 2
        loop(2, lambda k: log_tiles(earlier2, later2, log2, top, 0, points, half * width + k * part, part))
        stat[half] = jnp.max(top[:, span(half, width)], axis=0, keepdims=True)
        stat_out(2, peaks2, half)

    peaks_out_2(0)
    loop(HALVES, lambda half: stat_finish(dens1.at[half], recv_stat.at[1, half], density1, half, jnp.add))
    scale(v1, density1, scaled)
    product_send(me, scaled, kern, part1, arrived1, sum_sent_x.at[0], recv_x.at[0])

    def dens_out_2(half):
        stat_finish(peaks2.at[half], recv_stat.at[2, half], peak, half, jnp.maximum)
        exp_pass(log2, kern, peak, stat.at[half], half)
        stat_out(3, dens2, half)

    peaks_out_2(1)
    sum_send(me, arrived1, sums1, final1, sum_sent_z.at[0], recv_x.at[0], recv_z.at[0])
    loop(HALVES, dens_out_2)
    sum_own(me, arrived1, final1, recv_x.at[0])
    held = sum_finish(final1, recv_z.at[0])
    out_next[...] = held
    value_next = jnp.maximum(pay_next[...].astype(F32), held)
    own_v[1] = value_next
    v2[me.row] = value_next
    row_send(me, own_v.at[1], v2, *g(5))

    loop(HALVES, lambda half: stat_finish(dens2.at[half], recv_stat.at[3, half], density2, half, jnp.add))
    row_relay(me, v2, *g(5))
    row_finish(me, v2, recv_gather.at[5], lambda k: None)
    scale(v2, density2, scaled)
    product_send(me, scaled, kern, part2, arrived2, sum_sent_x.at[1], recv_x.at[1])
    sum_send(me, arrived2, sums2, final2, sum_sent_z.at[1], recv_x.at[1], recv_z.at[1])
    sum_own(me, arrived2, final2, recv_x.at[1])
    out_now[...] = sum_finish(final2, recv_z.at[1])

    for k, buf in ((0, x1), (1, y1), (2, x2), (3, y2), (4, v1), (5, v2)):
        wait_for(buf.at[pl.ds(0, SIDE - 1)], gather_send.at[k])
    for k, buf in ((0, peaks1), (1, dens1), (2, peaks2), (3, dens2)):
        for half in range(HALVES):
            wait_for(buf.at[half, pl.ds(0, SIDE - 1)], stat_sent.at[k, half])
    for k, part, final in ((0, part1, final1), (1, part2, final2)):
        wait_for(part.at[pl.ds(0, QUAD - 1)], sum_sent_x.at[k])
        wait_for(final.at[pl.ds(0, QUAD - 1)], sum_sent_z.at[k])


def per_device(states_now, states_next, states_last, payoff_now, payoff_next, payoff_last):
    factors, width = states_now.shape
    swaps = payoff_now.shape[0]
    points = SIDE * width
    states = pltpu.VMEM((SIDE, factors, width), F32)
    values = pltpu.VMEM((SIDE, swaps, width), F32)
    stats = pltpu.VMEM((HALVES, SIDE, 1, points // HALVES), F32)
    line = pltpu.VMEM((HALVES, 1, points // HALVES), F32)
    quad = pltpu.VMEM((QUAD, swaps, width), F32)
    square = pltpu.VMEM((QUAD, QUAD, swaps, width), F32)
    payoff = pltpu.VMEM((swaps, width), BF16)
    dma = pltpu.SemaphoreType.DMA
    vmem = pl.BlockSpec(memory_space=pltpu.VMEM)
    out = jax.ShapeDtypeStruct((swaps, width), F32)
    held_next, held_now = pl.pallas_call(
        kernel_body,
        out_shape=(out, out),
        in_specs=[pl.BlockSpec(memory_space=pl.ANY)] * 5,
        out_specs=(vmem, vmem),
        scratch_shapes=[states] * 4
        + [values, values, pltpu.VMEM((2, swaps, width), F32), payoff, payoff]
        + [pltpu.VMEM((points, 256), BF16), pltpu.VMEM((256, points), BF16)] * 2
        + [pltpu.VMEM((points, points), F32)] * 2
        + [pltpu.VMEM((points, points), BF16), pltpu.VMEM((swaps, points), BF16)]
        + [stats] * 4
        + [line] * 4
        + [pltpu.VMEM((8, points), F32)]
        + [square, square, quad, quad] * 2
        + [dma((6,)), dma((6,)), dma((4, HALVES)), dma((2,)), dma((2,))]
        + [dma((6, SIDE)), dma((4, HALVES)), dma((2, QUAD)), dma((2,))],
        compiler_params=pltpu.CompilerParams(
            collective_id=0, has_side_effects=True, vmem_limit_bytes=60 * 2**20
        ),
    )(states_now, states_next, states_last, payoff_next, payoff_last)
    return jnp.maximum(payoff_next.astype(F32), held_next), jnp.maximum(payoff_now.astype(F32), held_now)


def solution(mesh):
    early, late = P(None, ("row", "col")), P(None, ("col", "row"))
    return jax.shard_map(
        per_device,
        mesh=mesh,
        in_specs=(late, early, late, late, early, late),
        out_specs=(early, late),
        check_vma=False,
    )
```

```python
import jax
import jax.numpy as jnp
from jax import lax
from jax.experimental import pallas as pl
from jax.experimental.pallas import tpu as pltpu
from jax.sharding import PartitionSpec as P

F32, BF16 = jnp.float32, jnp.bfloat16
W = 128
SIDE = 16
QUAD = 4
HALVES = 2
HALF = 8
MESH = pl.DeviceIdType.MESH


def span(block, width):
    return pl.ds(pl.multiple_of(block * width, width), width)


def loop(count, body):
    def step(k, carry):
        body(k)
        return carry

    lax.fori_loop(0, count, step, 0)


def split3(v):
    high = v.astype(BF16).astype(F32)
    rest = v - high
    mid = rest.astype(BF16).astype(F32)
    return high, mid, rest - mid


def operand(block, earlier):
    high, mid, low = split3(block)
    norm = split3(-0.5 * jnp.sum(block * block, axis=0, keepdims=True))
    row = lax.broadcasted_iota(jnp.int32, (8, block.shape[1]), 0)
    extra = jnp.where(row < 6, 1.0, 0.0)
    for k in range(3):
        extra = jnp.where(row == (k if earlier else k + 3), norm[k], extra)
    pieces = (high, high, mid, mid, high, low) if earlier else (high, mid, high, mid, low, high)
    return jnp.concatenate(pieces + (extra, jnp.zeros_like(extra)), axis=0)


def build_later(states, later, k):
    later[:, span(k, W)] = operand(states[k], False).astype(BF16)


def build_earlier(states, earlier, k):
    earlier[span(k, W), :] = operand(states[k], True).T.astype(BF16)


def log_tiles(earlier, later, log_kernel, top, first_row, rows, first_col, cols):
    tile_rows, tile_cols = 256, 256
    for jc in range(cols // tile_cols):
        js = pl.ds(pl.multiple_of(first_col + jc * tile_cols, tile_cols), tile_cols)
        highest = top[:, js]
        for ic in range(rows // tile_rows):
            i = pl.ds(pl.multiple_of(first_row + ic * tile_rows, tile_rows), tile_rows)
            tile = jnp.dot(earlier[i, :], later[:, js], preferred_element_type=F32)
            log_kernel[i, js] = tile
            highest = jnp.maximum(highest, jnp.max(tile.reshape(tile_rows // 8, 8, tile_cols), axis=0))
        top[:, js] = highest


def exp_pass(log_kernel, top, stat, half):
    rows, cols = 64, 256
    blocks = log_kernel.shape[1] // cols // HALVES

    def col(jc):
        js = span(half * blocks + jc, cols)
        peak = jnp.max(top[:, js], axis=0, keepdims=True)
        stat[0, :, span(jc, cols)] = peak
        peak = jnp.broadcast_to(peak, (8, cols))

        def row(ic, total):
            i = span(ic, rows)
            tile = jnp.exp(log_kernel[i, js].reshape(rows // 8, 8, cols) - peak[None])
            log_kernel[i, js] = tile.reshape(rows, cols)
            return total + jnp.sum(tile, axis=0)

        count = log_kernel.shape[0] // rows
        total = lax.fori_loop(0, count, row, jnp.zeros((8, cols), F32), unroll=True)
        stat[1, :, span(jc, cols)] = jnp.sum(total, axis=0, keepdims=True)

    loop(blocks, col)


def kernel_tile(weights, factor, kernel, group):
    rows, cols = QUAD * W, 512
    blocks = kernel.shape[1] // cols

    def col(jc):
        part = blocks // HALVES
        own = jnp.broadcast_to(factor[jc // part, :, span(jc % part, cols)], (8, cols))
        js = span(jc, cols)
        piece = weights[span(group, rows), js].reshape(rows // 8, 8, cols) * own[None]
        kernel[span(group, rows), js] = piece.reshape(rows, cols).astype(BF16)

    loop(blocks, col)


def scale(values, density, scaled):
    loop(SIDE, lambda k: scale_block(values, density, scaled, k))


def scale_block(values, density, scaled, k):
    blocks = SIDE // HALVES
    below = density[k // blocks, :, span(k % blocks, W)]
    scaled[:, span(k, W)] = (values[k] / below).astype(BF16)


def remote(src, dst, send, recv, row, col):
    return pltpu.make_async_remote_copy(
        src_ref=src, dst_ref=dst, send_sem=send, recv_sem=recv, device_id=(row, col), device_id_type=MESH
    )


def wait_for(ref, sem):
    pltpu.make_async_copy(ref, ref, sem).wait()


class Place:
    def __init__(self):
        self.row, self.col = lax.axis_index("row"), lax.axis_index("col")
        self.chip, self.core = self.row // 2, self.row % 2
        self.low, self.y = self.chip // QUAD, self.chip % QUAD
        self.z, self.x = self.col // QUAD, self.col % QUAD
        self.twin = self.chip * 2 + 1 - self.core

    def on_core(self, k, other=0):
        core = 1 - self.core if other else self.core
        return (((self.low + k // QUAD) % 2) * QUAD + (self.y + near(k % QUAD)) % QUAD) * 2 + core

    def along_z(self, k):
        return ((self.z + k) % QUAD) * QUAD + self.x

    def along_x(self, k):
        return self.z * QUAD + (self.x + k) % QUAD


def near(k):
    return k + k // 2 - 2 * (k // 3)


def far(k):
    return 2 - k + 3 * (k // 2) - 2 * (k // 3)


def row_send(me, own, buf, send, recv):
    def one(k):
        remote(own, buf.at[me.row], send, recv.at[me.row], me.on_core(HALF - 1 - k), me.col).start()

    loop(HALF - 1, one)
    remote(own, buf.at[me.row], send, recv.at[me.row], me.twin, me.col).start()


def row_relay(me, buf, send, recv):
    def one(k):
        slot = me.on_core(k + 1)
        wait_for(buf.at[slot], recv.at[slot])
        remote(buf.at[slot], buf.at[slot], send, recv.at[slot], me.twin, me.col).start()

    loop(HALF - 1, one)


def row_finish(me, buf, recv, then):
    def one(k):
        then(me.on_core(k))
        slot = me.on_core(k, other=1)
        wait_for(buf.at[slot], recv.at[slot])
        then(slot)

    loop(HALF, one)


def col_send(me, own, buf, send, recv):
    def along_z(k):
        remote(own, buf.at[me.col], send, recv.at[me.col], me.row, me.along_z(far(k))).start()

    def along_x(k):
        remote(own, buf.at[me.col], send, recv.at[me.col], me.row, me.along_x(far(k))).start()

    loop(QUAD - 1, along_z)
    loop(QUAD - 1, along_x)


def col_relay(me, buf, send, recv):
    def one(k):
        slot = me.along_z(near(k + 1))
        wait_for(buf.at[slot], recv.at[slot])

        def two(q):
            remote(buf.at[slot], buf.at[slot], send, recv.at[slot], me.row, me.along_x(far(q))).start()

        loop(QUAD - 1, two)

    loop(QUAD - 1, one)


def col_finish(me, buf, recv, k, then):
    group = (me.z + k) % QUAD
    then(group * QUAD + me.x)

    def one(q):
        slot = group * QUAD + (me.x + near(q + 1)) % QUAD
        wait_for(buf.at[slot], recv.at[slot])
        then(slot)

    loop(QUAD - 1, one)
    return group


def stat_send(me, stat, buf, send, recv):
    buf[me.row] = stat[...]
    own = buf.at[me.row]

    def one(k):
        remote(own, own, send, recv, (me.row + k + 1) % SIDE, me.col).start()

    loop(SIDE - 1, one)


def stat_finish(me, buf, recv, factor, density, half):
    wait_for(buf.at[pl.ds(0, SIDE - 1)], recv)
    peak = buf[0, 0]
    for k in range(1, SIDE):
        peak = jnp.maximum(peak, buf[k, 0])
    total = buf[0, 1] * jnp.exp(buf[0, 0] - peak)
    for k in range(1, SIDE):
        total = total + buf[k, 1] * jnp.exp(buf[k, 0] - peak)
    density[half] = total
    factor[half] = jnp.exp(buf[me.row, 0] - peak)


def product_send(me, scaled, kernel, form, part, arrived, send, recv):
    def zs(k):
        z = (me.z + far(k)) % QUAD
        if form:
            form(z)
        product = lax.dot_general(scaled[...], kernel[span(z, QUAD * W), :], (((1,), (1,)), ((), ())), preferred_element_type=F32)
        for x in range(QUAD):
            part[z, x] = product[:, x * W : (x + 1) * W]

        def away(q):
            x = (me.x + far(q)) % QUAD
            remote(part.at[z, x], arrived.at[z, me.x], send, recv.at[z], me.row, me.z * QUAD + x).start()

        loop(QUAD - 1, away)
        arrived[z, me.x] = part[z, me.x]

    loop(QUAD, zs)


def sum_send(me, arrived, sums, final, send, recv_x, recv_z):
    def one(k):
        z = (me.z + far(k)) % QUAD
        wait_for(arrived.at[z, pl.ds(0, QUAD - 1)], recv_x.at[z])
        sums[z] = arrived[z, 0] + arrived[z, 1] + arrived[z, 2] + arrived[z, 3]
        remote(sums.at[z], final.at[me.z], send, recv_z, me.row, z * QUAD + me.x).start()

    loop(QUAD - 1, one)


def sum_own(me, arrived, final, recv_x):
    wait_for(arrived.at[me.z, pl.ds(0, QUAD - 1)], recv_x.at[me.z])
    final[me.z] = arrived[me.z, 0] + arrived[me.z, 1] + arrived[me.z, 2] + arrived[me.z, 3]


def sum_finish(final, recv_z):
    wait_for(final.at[pl.ds(0, QUAD - 1)], recv_z)
    return final[0] + final[1] + final[2] + final[3]


def kernel_body(
    now_ref, next_ref, last_ref, pay_next_ref, pay_last_ref, out_next, out_now,
    x1, y1, x2, y2, v1, v2, own_v, pay_next, pay_last,
    earlier1, later1, earlier2, later2, log1, log2, kern, scaled,
    stats1, stats2, factor1, factor2, density1, density2, stat, top,
    part1, arrived1, sums1, final1, part2, arrived2, sums2, final2,
    own_sem, gather_send, stat_sent, sum_sent_x, sum_sent_z,
    recv_gather, recv_stat, recv_x, recv_z,
):
    me = Place()
    points, width = log1.shape[1], stat.shape[3]

    barrier = pltpu.get_barrier_semaphore()

    def greet_col(k):
        pl.semaphore_signal(barrier, inc=1, device_id=(me.row, me.along_z(k + 1)), device_id_type=MESH)
        pl.semaphore_signal(barrier, inc=1, device_id=(me.row, me.along_x(k + 1)), device_id_type=MESH)

    loop(QUAD - 1, greet_col)

    def greet_row(k):
        pl.semaphore_signal(barrier, inc=1, device_id=((me.row + k + 1) % SIDE, me.col), device_id_type=MESH)

    loop(SIDE - 1, greet_row)

    own = [
        pltpu.make_async_copy(src, dst, own_sem.at[k])
        for k, (src, dst) in enumerate(
            (
                (next_ref, x1.at[me.col]),
                (last_ref, y1.at[me.row]),
                (now_ref, x2.at[me.col]),
                (next_ref, y2.at[me.row]),
                (pay_next_ref, pay_next),
                (pay_last_ref, pay_last),
            )
        )
    ]
    for copy in own:
        copy.start()
    for copy in own:
        copy.wait()
    own_v[0] = pay_last[...].astype(F32)
    v1[me.row] = own_v[0]
    top[...] = jnp.full_like(top, -jnp.inf)
    pl.semaphore_wait(barrier, SIDE - 1 + 2 * (QUAD - 1))

    g = lambda k: (gather_send.at[k], recv_gather.at[k])
    add_x1 = lambda k: build_earlier(x1, earlier1, k)
    add_y1 = lambda k: build_later(y1, later1, k)
    add_x2 = lambda k: build_earlier(x2, earlier2, k)
    add_y2 = lambda k: build_later(y2, later2, k)

    col_send(me, x1.at[me.col], x1, *g(0))
    row_send(me, y1.at[me.row], y1, *g(1))
    row_relay(me, y1, *g(1))
    col_relay(me, x1, *g(0))
    row_send(me, own_v.at[0], v1, *g(4))
    row_send(me, y2.at[me.row], y2, *g(3))
    col_send(me, x2.at[me.col], x2, *g(2))
    row_finish(me, y1, recv_gather.at[1], add_y1)

    def group_in(k):
        group = col_finish(me, x1, recv_gather.at[0], near(k), add_x1)
        log_tiles(earlier1, later1, log1, top, group * QUAD * W, QUAD * W, 0, points)

    def stat_out(k, buf, half):
        stat_send(me, stat.at[half], buf.at[half], stat_sent.at[k, half], recv_stat.at[k, half])

    def stats_out(half):
        log_tiles(earlier1, later1, log1, top, last * QUAD * W, QUAD * W, half * width, width)
        exp_pass(log1, top, stat.at[half], half)
        stat_out(0, stats1, half)

    loop(QUAD - 1, group_in)
    last = col_finish(me, x1, recv_gather.at[0], 2, add_x1)
    loop(HALVES, stats_out)
    top[...] = jnp.full_like(top, -jnp.inf)

    row_relay(me, v1, *g(4))
    row_relay(me, y2, *g(3))
    col_relay(me, x2, *g(2))
    row_finish(me, y2, recv_gather.at[3], add_y2)

    loop(QUAD, lambda k: (col_finish(me, x2, recv_gather.at[2], near(k), add_x2), None)[1])
    row_finish(me, v1, recv_gather.at[4], lambda k: None)

    def log_2(half):
        part = width // 2
        loop(2, lambda k: log_tiles(earlier2, later2, log2, top, 0, points, half * width + k * part, part))

    def stats_out_2(half):
        exp_pass(log2, top, stat.at[half], half)
        stat_out(1, stats2, half)

    log_2(0)
    loop(HALVES, lambda half: stat_finish(me, stats1.at[half], recv_stat.at[0, half], factor1, density1, half))
    scale(v1, density1, scaled)
    product_send(me, scaled, kern, lambda z: kernel_tile(log1, factor1, kern, z), part1, arrived1, sum_sent_x.at[0], recv_x.at[0])
    log_2(1)
    sum_send(me, arrived1, sums1, final1, sum_sent_z.at[0], recv_x.at[0], recv_z.at[0])
    loop(HALVES, stats_out_2)
    sum_own(me, arrived1, final1, recv_x.at[0])
    held = sum_finish(final1, recv_z.at[0])
    out_next[...] = held
    value_next = jnp.maximum(pay_next[...].astype(F32), held)
    own_v[1] = value_next
    v2[me.row] = value_next
    row_send(me, own_v.at[1], v2, *g(5))

    loop(HALVES, lambda half: stat_finish(me, stats2.at[half], recv_stat.at[1, half], factor2, density2, half))
    row_relay(me, v2, *g(5))
    loop(QUAD, lambda z: kernel_tile(log2, factor2, kern, z))
    row_finish(me, v2, recv_gather.at[5], lambda k: scale_block(v2, density2, scaled, k))
    product_send(me, scaled, kern, None, part2, arrived2, sum_sent_x.at[1], recv_x.at[1])
    sum_send(me, arrived2, sums2, final2, sum_sent_z.at[1], recv_x.at[1], recv_z.at[1])
    sum_own(me, arrived2, final2, recv_x.at[1])
    out_now[...] = sum_finish(final2, recv_z.at[1])

    for k, buf in ((0, x1), (1, y1), (2, x2), (3, y2), (4, v1), (5, v2)):
        wait_for(buf.at[pl.ds(0, SIDE - 1)], gather_send.at[k])
    for k, buf in ((0, stats1), (1, stats2)):
        for half in range(HALVES):
            wait_for(buf.at[half, pl.ds(0, SIDE - 1)], stat_sent.at[k, half])
    for k, part, final in ((0, part1, final1), (1, part2, final2)):
        wait_for(part.at[pl.ds(0, QUAD - 1)], sum_sent_x.at[k])
        wait_for(final.at[pl.ds(0, QUAD - 1)], sum_sent_z.at[k])


def per_device(states_now, states_next, states_last, payoff_now, payoff_next, payoff_last):
    factors, width = states_now.shape
    swaps = payoff_now.shape[0]
    points = SIDE * width
    states = pltpu.VMEM((SIDE, factors, width), F32)
    values = pltpu.VMEM((SIDE, swaps, width), F32)
    stats = pltpu.VMEM((HALVES, SIDE, 2, 1, points // HALVES), F32)
    line = pltpu.VMEM((HALVES, 1, points // HALVES), F32)
    quad = pltpu.VMEM((QUAD, swaps, width), F32)
    square = pltpu.VMEM((QUAD, QUAD, swaps, width), F32)
    payoff = pltpu.VMEM((swaps, width), BF16)
    dma = pltpu.SemaphoreType.DMA
    vmem = pl.BlockSpec(memory_space=pltpu.VMEM)
    out = jax.ShapeDtypeStruct((swaps, width), F32)
    held_next, held_now = pl.pallas_call(
        kernel_body,
        out_shape=(out, out),
        in_specs=[pl.BlockSpec(memory_space=pl.ANY)] * 5,
        out_specs=(vmem, vmem),
        scratch_shapes=[states] * 4
        + [values, values, pltpu.VMEM((2, swaps, width), F32), payoff, payoff]
        + [pltpu.VMEM((points, 256), BF16), pltpu.VMEM((256, points), BF16)] * 2
        + [pltpu.VMEM((points, points), F32)] * 2
        + [pltpu.VMEM((points, points), BF16), pltpu.VMEM((swaps, points), BF16)]
        + [stats] * 2
        + [line] * 4
        + [pltpu.VMEM((HALVES, 2, 1, points // HALVES), F32)]
        + [pltpu.VMEM((8, points), F32)]
        + [square, square, quad, quad] * 2
        + [dma((6,)), dma((6,)), dma((2, HALVES)), dma((2,)), dma((2,))]
        + [dma((6, SIDE)), dma((2, HALVES)), dma((2, QUAD)), dma((2,))],
        compiler_params=pltpu.CompilerParams(
            collective_id=0, has_side_effects=True, vmem_limit_bytes=60 * 2**20
        ),
    )(states_now, states_next, states_last, payoff_next, payoff_last)
    return jnp.maximum(payoff_next.astype(F32), held_next), jnp.maximum(payoff_now.astype(F32), held_now)


def solution(mesh):
    early, late = P(None, ("row", "col")), P(None, ("col", "row"))
    return jax.shard_map(
        per_device,
        mesh=mesh,
        in_specs=(late, early, late, late, early, late),
        out_specs=(early, late),
        check_vma=False,
    )
```

```python
import jax
import jax.numpy as jnp
from jax import lax
from jax.experimental import pallas as pl
from jax.experimental.pallas import tpu as pltpu
from jax.sharding import PartitionSpec as P

F32, BF16 = jnp.float32, jnp.bfloat16
W = 128
SIDE = 16
QUAD = 4
PARTS = 4
HALF = 8
MESH = pl.DeviceIdType.MESH


def span(block, width):
    return pl.ds(pl.multiple_of(block * width, width), width)


def loop(count, body):
    def step(k, carry):
        body(k)
        return carry

    lax.fori_loop(0, count, step, 0)


def split3(v):
    high = v.astype(BF16).astype(F32)
    rest = v - high
    mid = rest.astype(BF16).astype(F32)
    return high, mid, rest - mid


def operand(block, earlier):
    high, mid, low = split3(block)
    norm = split3(-0.5 * jnp.sum(block * block, axis=0, keepdims=True))
    row = lax.broadcasted_iota(jnp.int32, (8, block.shape[1]), 0)
    extra = jnp.where(row < 6, 1.0, 0.0)
    for k in range(3):
        extra = jnp.where(row == (k if earlier else k + 3), norm[k], extra)
    pieces = (high, high, mid, mid, high, low) if earlier else (high, mid, high, mid, low, high)
    return jnp.concatenate(pieces + (extra, jnp.zeros_like(extra)), axis=0)


def build_later(states, later, k):
    later[:, span(k, W)] = operand(states[k], False).astype(BF16)


def build_earlier(states, earlier, k):
    earlier[span(k, W), :] = operand(states[k], True).T.astype(BF16)


def log_tiles(earlier, later, log_kernel, top, first_row, rows, first_col, cols):
    tile_rows, tile_cols = 256, 256
    for jc in range(cols // tile_cols):
        js = pl.ds(pl.multiple_of(first_col + jc * tile_cols, tile_cols), tile_cols)
        highest = top[:, js]
        for ic in range(rows // tile_rows):
            i = pl.ds(pl.multiple_of(first_row + ic * tile_rows, tile_rows), tile_rows)
            tile = jnp.dot(earlier[i, :], later[:, js], preferred_element_type=F32)
            log_kernel[i, js] = tile
            highest = jnp.maximum(highest, jnp.max(tile.reshape(tile_rows // 8, 8, tile_cols), axis=0))
        top[:, js] = highest


def exp_pass(log_kernel, top, stat, part_at):
    rows, cols = 64, 256
    blocks = log_kernel.shape[1] // cols // PARTS

    def col(jc):
        js = span(part_at * blocks + jc, cols)
        peak = jnp.max(top[:, js], axis=0, keepdims=True)
        stat[0, :, span(jc, cols)] = peak
        peak = jnp.broadcast_to(peak, (8, cols))

        def row(ic, total):
            i = span(ic, rows)
            tile = jnp.exp(log_kernel[i, js].reshape(rows // 8, 8, cols) - peak[None])
            log_kernel[i, js] = tile.reshape(rows, cols)
            return total + jnp.sum(tile, axis=0)

        count = log_kernel.shape[0] // rows
        total = lax.fori_loop(0, count, row, jnp.zeros((8, cols), F32), unroll=True)
        stat[1, :, span(jc, cols)] = jnp.sum(total, axis=0, keepdims=True)

    loop(blocks, col)


def kernel_tile(weights, factor, kernel, group):
    rows, cols = QUAD * W, 512
    blocks = kernel.shape[1] // cols

    def col(jc):
        part = blocks // PARTS
        own = jnp.broadcast_to(factor[jc // part, :, span(jc % part, cols)], (8, cols))
        js = span(jc, cols)
        piece = weights[span(group, rows), js].reshape(rows // 8, 8, cols) * own[None]
        kernel[span(group, rows), js] = piece.reshape(rows, cols).astype(BF16)

    loop(blocks, col)


def scale(values, density, scaled):
    loop(SIDE, lambda k: scale_block(values, density, scaled, k))


def scale_block(values, density, scaled, k):
    blocks = SIDE // PARTS
    below = density[k // blocks, :, span(k % blocks, W)]
    scaled[:, span(k, W)] = (values[k] / below).astype(BF16)


def remote(src, dst, send, recv, row, col):
    return pltpu.make_async_remote_copy(
        src_ref=src, dst_ref=dst, send_sem=send, recv_sem=recv, device_id=(row, col), device_id_type=MESH
    )


def wait_for(ref, sem):
    pltpu.make_async_copy(ref, ref, sem).wait()


class Place:
    def __init__(self):
        self.row, self.col = lax.axis_index("row"), lax.axis_index("col")
        self.chip, self.core = self.row // 2, self.row % 2
        self.low, self.y = self.chip // QUAD, self.chip % QUAD
        self.z, self.x = self.col // QUAD, self.col % QUAD
        self.twin = self.chip * 2 + 1 - self.core

    def on_core(self, k, other=0):
        core = 1 - self.core if other else self.core
        return (((self.low + k // QUAD) % 2) * QUAD + (self.y + near(k % QUAD)) % QUAD) * 2 + core

    def along_z(self, k):
        return ((self.z + k) % QUAD) * QUAD + self.x

    def along_x(self, k):
        return self.z * QUAD + (self.x + k) % QUAD


def near(k):
    return k + k // 2 - 2 * (k // 3)


def far(k):
    return 2 - k + 3 * (k // 2) - 2 * (k // 3)


def row_send(me, own, buf, send, recv):
    def one(k):
        remote(own, buf.at[me.row], send, recv.at[me.row], me.on_core(HALF - 1 - k), me.col).start()

    loop(HALF - 1, one)
    remote(own, buf.at[me.row], send, recv.at[me.row], me.twin, me.col).start()


def row_relay(me, buf, send, recv):
    def one(k):
        slot = me.on_core(k + 1)
        wait_for(buf.at[slot], recv.at[slot])
        remote(buf.at[slot], buf.at[slot], send, recv.at[slot], me.twin, me.col).start()

    loop(HALF - 1, one)


def row_finish(me, buf, recv, then):
    def one(k):
        then(me.on_core(k))
        slot = me.on_core(k, other=1)
        wait_for(buf.at[slot], recv.at[slot])
        then(slot)

    loop(HALF, one)


def col_send(me, own, buf, send, recv):
    def along_z(k):
        remote(own, buf.at[me.col], send, recv.at[me.col], me.row, me.along_z(far(k))).start()

    def along_x(k):
        remote(own, buf.at[me.col], send, recv.at[me.col], me.row, me.along_x(far(k))).start()

    loop(QUAD - 1, along_z)
    loop(QUAD - 1, along_x)


def col_relay(me, buf, send, recv):
    def one(k):
        slot = me.along_z(near(k + 1))
        wait_for(buf.at[slot], recv.at[slot])

        def two(q):
            remote(buf.at[slot], buf.at[slot], send, recv.at[slot], me.row, me.along_x(far(q))).start()

        loop(QUAD - 1, two)

    loop(QUAD - 1, one)


def col_finish(me, buf, recv, k, then):
    group = (me.z + k) % QUAD
    then(group * QUAD + me.x)

    def one(q):
        slot = group * QUAD + (me.x + near(q + 1)) % QUAD
        wait_for(buf.at[slot], recv.at[slot])
        then(slot)

    loop(QUAD - 1, one)
    return group


def stat_send(me, stat, buf, send, recv):
    buf[me.row] = stat[...]
    own = buf.at[me.row]

    def one(k):
        remote(own, own, send, recv, (me.row + k + 1) % SIDE, me.col).start()

    loop(SIDE - 1, one)


def stat_finish(me, buf, recv, factor, density, part_at):
    wait_for(buf.at[pl.ds(0, SIDE - 1)], recv)
    peak = buf[0, 0]
    for k in range(1, SIDE):
        peak = jnp.maximum(peak, buf[k, 0])
    total = buf[0, 1] * jnp.exp(buf[0, 0] - peak)
    for k in range(1, SIDE):
        total = total + buf[k, 1] * jnp.exp(buf[k, 0] - peak)
    density[part_at] = total
    factor[part_at] = jnp.exp(buf[me.row, 0] - peak)


def product_send(me, scaled, kernel, form, part, arrived, send, recv):
    def zs(k):
        z = (me.z + far(k)) % QUAD
        if form:
            form(z)
        product = lax.dot_general(scaled[...], kernel[span(z, QUAD * W), :], (((1,), (1,)), ((), ())), preferred_element_type=F32)
        for x in range(QUAD):
            part[z, x] = product[:, x * W : (x + 1) * W]

        def away(q):
            x = (me.x + far(q)) % QUAD
            remote(part.at[z, x], arrived.at[z, me.x], send, recv.at[z], me.row, me.z * QUAD + x).start()

        loop(QUAD - 1, away)
        arrived[z, me.x] = part[z, me.x]

    loop(QUAD, zs)


def sum_send(me, arrived, sums, final, send, recv_x, recv_z):
    def one(k):
        z = (me.z + far(k)) % QUAD
        wait_for(arrived.at[z, pl.ds(0, QUAD - 1)], recv_x.at[z])
        sums[z] = arrived[z, 0] + arrived[z, 1] + arrived[z, 2] + arrived[z, 3]
        remote(sums.at[z], final.at[me.z], send, recv_z, me.row, z * QUAD + me.x).start()

    loop(QUAD - 1, one)


def sum_own(me, arrived, final, recv_x):
    wait_for(arrived.at[me.z, pl.ds(0, QUAD - 1)], recv_x.at[me.z])
    final[me.z] = arrived[me.z, 0] + arrived[me.z, 1] + arrived[me.z, 2] + arrived[me.z, 3]


def sum_finish(final, recv_z):
    wait_for(final.at[pl.ds(0, QUAD - 1)], recv_z)
    return final[0] + final[1] + final[2] + final[3]


def kernel_body(
    now_ref, next_ref, last_ref, pay_next_ref, pay_last_ref, out_next, out_now,
    x1, y1, x2, y2, v1, v2, own_v, pay_next, pay_last,
    earlier1, later1, earlier2, later2, log1, log2, kern, scaled,
    stats1, stats2, factor1, factor2, density1, density2, stat, top,
    part1, arrived1, sums1, final1, part2, arrived2, sums2, final2,
    own_sem, gather_send, stat_sent, sum_sent_x, sum_sent_z,
    recv_gather, recv_stat, recv_x, recv_z,
):
    me = Place()
    points, width = log1.shape[1], stat.shape[3]

    barrier = pltpu.get_barrier_semaphore()

    def greet_col(k):
        pl.semaphore_signal(barrier, inc=1, device_id=(me.row, me.along_z(k + 1)), device_id_type=MESH)
        pl.semaphore_signal(barrier, inc=1, device_id=(me.row, me.along_x(k + 1)), device_id_type=MESH)

    loop(QUAD - 1, greet_col)

    def greet_row(k):
        pl.semaphore_signal(barrier, inc=1, device_id=((me.row + k + 1) % SIDE, me.col), device_id_type=MESH)

    loop(SIDE - 1, greet_row)

    own = [
        pltpu.make_async_copy(src, dst, own_sem.at[k])
        for k, (src, dst) in enumerate(
            (
                (next_ref, x1.at[me.col]),
                (last_ref, y1.at[me.row]),
                (now_ref, x2.at[me.col]),
                (next_ref, y2.at[me.row]),
                (pay_next_ref, pay_next),
                (pay_last_ref, pay_last),
            )
        )
    ]
    for copy in own:
        copy.start()
    for copy in own:
        copy.wait()
    own_v[0] = pay_last[...].astype(F32)
    v1[me.row] = own_v[0]
    top[...] = jnp.full_like(top, -jnp.inf)
    pl.semaphore_wait(barrier, SIDE - 1 + 2 * (QUAD - 1))

    g = lambda k: (gather_send.at[k], recv_gather.at[k])
    add_x1 = lambda k: build_earlier(x1, earlier1, k)
    add_y1 = lambda k: build_later(y1, later1, k)
    add_x2 = lambda k: build_earlier(x2, earlier2, k)
    add_y2 = lambda k: build_later(y2, later2, k)

    col_send(me, x1.at[me.col], x1, *g(0))
    row_send(me, y1.at[me.row], y1, *g(1))
    row_relay(me, y1, *g(1))
    col_relay(me, x1, *g(0))
    row_send(me, own_v.at[0], v1, *g(4))
    row_send(me, y2.at[me.row], y2, *g(3))
    col_send(me, x2.at[me.col], x2, *g(2))
    row_finish(me, y1, recv_gather.at[1], add_y1)

    def group_in(k):
        group = col_finish(me, x1, recv_gather.at[0], near(k), add_x1)
        log_tiles(earlier1, later1, log1, top, group * QUAD * W, QUAD * W, 0, points)

    def stat_out(k, buf, part_at):
        stat_send(me, stat.at[part_at], buf.at[part_at], stat_sent.at[k, part_at], recv_stat.at[k, part_at])

    def stats_out(part_at):
        log_tiles(earlier1, later1, log1, top, last * QUAD * W, QUAD * W, part_at * width, width)
        exp_pass(log1, top, stat.at[part_at], part_at)
        stat_out(0, stats1, part_at)

    loop(QUAD - 1, group_in)
    last = col_finish(me, x1, recv_gather.at[0], 2, add_x1)
    loop(PARTS, stats_out)
    top[...] = jnp.full_like(top, -jnp.inf)

    row_relay(me, v1, *g(4))
    row_relay(me, y2, *g(3))
    col_relay(me, x2, *g(2))
    row_finish(me, y2, recv_gather.at[3], add_y2)

    loop(QUAD, lambda k: (col_finish(me, x2, recv_gather.at[2], near(k), add_x2), None)[1])
    row_finish(me, v1, recv_gather.at[4], lambda k: None)

    def log_2(part_at):
        part = width // 2
        loop(2, lambda k: log_tiles(earlier2, later2, log2, top, 0, points, part_at * width + k * part, part))

    def stats_out_2(part_at):
        exp_pass(log2, top, stat.at[part_at], part_at)
        stat_out(1, stats2, part_at)

    loop(PARTS // 2, log_2)
    loop(PARTS, lambda part_at: stat_finish(me, stats1.at[part_at], recv_stat.at[0, part_at], factor1, density1, part_at))
    scale(v1, density1, scaled)
    product_send(me, scaled, kern, lambda z: kernel_tile(log1, factor1, kern, z), part1, arrived1, sum_sent_x.at[0], recv_x.at[0])
    loop(PARTS // 2, lambda part: log_2(PARTS // 2 + part))
    sum_send(me, arrived1, sums1, final1, sum_sent_z.at[0], recv_x.at[0], recv_z.at[0])
    loop(PARTS, stats_out_2)
    sum_own(me, arrived1, final1, recv_x.at[0])
    held = sum_finish(final1, recv_z.at[0])
    out_next[...] = held
    value_next = jnp.maximum(pay_next[...].astype(F32), held)
    own_v[1] = value_next
    v2[me.row] = value_next
    row_send(me, own_v.at[1], v2, *g(5))

    loop(PARTS, lambda part_at: stat_finish(me, stats2.at[part_at], recv_stat.at[1, part_at], factor2, density2, part_at))
    row_relay(me, v2, *g(5))
    loop(QUAD, lambda z: kernel_tile(log2, factor2, kern, z))
    row_finish(me, v2, recv_gather.at[5], lambda k: scale_block(v2, density2, scaled, k))
    product_send(me, scaled, kern, None, part2, arrived2, sum_sent_x.at[1], recv_x.at[1])
    sum_send(me, arrived2, sums2, final2, sum_sent_z.at[1], recv_x.at[1], recv_z.at[1])
    sum_own(me, arrived2, final2, recv_x.at[1])
    out_now[...] = sum_finish(final2, recv_z.at[1])

    for k, buf in ((0, x1), (1, y1), (2, x2), (3, y2), (4, v1), (5, v2)):
        wait_for(buf.at[pl.ds(0, SIDE - 1)], gather_send.at[k])
    for k, buf in ((0, stats1), (1, stats2)):
        for part_at in range(PARTS):
            wait_for(buf.at[part_at, pl.ds(0, SIDE - 1)], stat_sent.at[k, part_at])
    for k, part, final in ((0, part1, final1), (1, part2, final2)):
        wait_for(part.at[pl.ds(0, QUAD - 1)], sum_sent_x.at[k])
        wait_for(final.at[pl.ds(0, QUAD - 1)], sum_sent_z.at[k])


def per_device(states_now, states_next, states_last, payoff_now, payoff_next, payoff_last):
    factors, width = states_now.shape
    swaps = payoff_now.shape[0]
    points = SIDE * width
    states = pltpu.VMEM((SIDE, factors, width), F32)
    values = pltpu.VMEM((SIDE, swaps, width), F32)
    stats = pltpu.VMEM((PARTS, SIDE, 2, 1, points // PARTS), F32)
    line = pltpu.VMEM((PARTS, 1, points // PARTS), F32)
    quad = pltpu.VMEM((QUAD, swaps, width), F32)
    square = pltpu.VMEM((QUAD, QUAD, swaps, width), F32)
    payoff = pltpu.VMEM((swaps, width), BF16)
    dma = pltpu.SemaphoreType.DMA
    vmem = pl.BlockSpec(memory_space=pltpu.VMEM)
    out = jax.ShapeDtypeStruct((swaps, width), F32)
    held_next, held_now = pl.pallas_call(
        kernel_body,
        out_shape=(out, out),
        in_specs=[pl.BlockSpec(memory_space=pl.ANY)] * 5,
        out_specs=(vmem, vmem),
        scratch_shapes=[states] * 4
        + [values, values, pltpu.VMEM((2, swaps, width), F32), payoff, payoff]
        + [pltpu.VMEM((points, 256), BF16), pltpu.VMEM((256, points), BF16)] * 2
        + [pltpu.VMEM((points, points), F32)] * 2
        + [pltpu.VMEM((points, points), BF16), pltpu.VMEM((swaps, points), BF16)]
        + [stats] * 2
        + [line] * 4
        + [pltpu.VMEM((PARTS, 2, 1, points // PARTS), F32)]
        + [pltpu.VMEM((8, points), F32)]
        + [square, square, quad, quad] * 2
        + [dma((6,)), dma((6,)), dma((2, PARTS)), dma((2,)), dma((2,))]
        + [dma((6, SIDE)), dma((2, PARTS)), dma((2, QUAD)), dma((2,))],
        compiler_params=pltpu.CompilerParams(
            collective_id=0, has_side_effects=True, vmem_limit_bytes=60 * 2**20
        ),
    )(states_now, states_next, states_last, payoff_next, payoff_last)
    return jnp.maximum(payoff_next.astype(F32), held_next), jnp.maximum(payoff_now.astype(F32), held_now)


def solution(mesh):
    early, late = P(None, ("row", "col")), P(None, ("col", "row"))
    return jax.shard_map(
        per_device,
        mesh=mesh,
        in_specs=(late, early, late, late, early, late),
        out_specs=(early, late),
        check_vma=False,
    )
```
